128 devices in a mesh: expert: 16 (over z, y), tensor: 8 (over x, core).
Axes of the slice: x: 4, y: 4, z: 4, core: 2. Of those that a mesh axis runs over, the one named last changes fastest.
Arguments:
- conv_input: bfloat16 [1024, 8192], P('expert', 'tensor'), may hold values from -6 to 6
- gate_input: bfloat16 [1024, 8192], P('expert', 'tensor'), may hold values from -6 to 6
- conv_cache: bfloat16 [320, 3, 8192], P('expert', None, 'tensor'), may hold values from -6 to 6
- state_cache: float32 [320, 16, 8192], P('expert', None, 'tensor'), may hold values from -6 to 6
- span_lengths: int32 [16, 4], P('expert'), may hold values from 1 to 28, 48 in all within a row
- span_resumes: int32 [16, 4], P('expert'), may hold values from 0 to 1
- slot_index: int32 [16, 20], P('expert'), may hold values from 0 to 19, each once within a row
- conv_weight: float32 [4, 8192], P(None, 'tensor'), may hold values from -3 to 3
- conv_bias: float32 [8192], P('tensor'), may hold values from -3 to 3
- rank_weight: bfloat16 [8192, 512], P('tensor'), may hold values from -0.0625 to 0.0625
- state_weight: bfloat16 [8192, 32], P('tensor'), may hold values from -0.0625 to 0.0625
- step_gain: float32 [512], replicated, may hold values from 0.1 to 1.9
- step_weight: bfloat16 [512, 8192], P(None, 'tensor'), may hold values from -0.25 to 0.25
- step_bias: float32 [8192], P('tensor'), may hold values from -6.9 to -2.3
- decay_log: float32 [16, 8192], P(None, 'tensor'), may hold values from 0 to 2.77
- skip_gain: float32 [8192], P('tensor'), may hold values from 0.5 to 1.5
- out_weight: bfloat16 [8192, 4096], P('tensor'), may hold values from -0.09375 to 0.09375
- residual: bfloat16 [1024, 4096], P('expert', 'tensor'), may hold values from -8 to 8
- moe_gain: float32 [4096], P('tensor'), may hold values from 0.1 to 1.9
- router_weight: bfloat16 [4096, 4], P('tensor'), may hold values from -0.09375 to 0.09375
- chosen_experts: int32 [1024, 2], P('expert'), may hold values from 0 to 3, all different within a row; in each aligned block of 64 rows (0 to 63, 64 to 127, ...) at most 48 rows name the same one
- gate_weight: bfloat16 [16, 4096, 3072], P('expert', None, 'tensor'), may hold values from -0.09375 to 0.09375
- up_weight: bfloat16 [16, 4096, 3072], P('expert', None, 'tensor'), may hold values from -0.09375 to 0.09375
- down_weight: bfloat16 [16, 3072, 4096], P('expert', 'tensor'), may hold values from -0.078125 to 0.078125
Outputs:
- mixed: bfloat16 [1024, 4096], P('expert', 'tensor')
- new_state_cache: float32 [320, 16, 8192], P('expert', None, 'tensor')
- new_conv_cache: bfloat16 [320, 3, 8192], P('expert', None, 'tensor')
The draws below stay inside these ranges and needn't reach their ends.
Inputs may be any that keep to these rules, and one draw needn't show every extreme that they name: `chosen_experts`: the rows of one row group name each expert at most 48 times; some expert is named exactly 48 times by some group; every expert is named somewhere. `span_lengths`: a group's 4 lengths sum to 48. `slot_index`: each group's row is an ordering of its 20 cache rows.
All inputs are finite; a program needn't handle non-finite values.
Results may differ from the reference program's by a relative error of at most 0.012.
Values may be sent and summed in bfloat16 or wider, within the bound.
No kernel may reach another device: no remote copies, remote signals or barrier semaphores. Data moves between devices by JAX's collectives and lax.ppermute only.
A program may use at most 128 MiB of HBM per device.

```python
import math
import jax
import jax.numpy as jnp
import numpy as np
from jax import lax

D = 4096
DI = 8192
NS = 16
R = 512
CONV = 4
FF = 12288
EXPERTS = 4
DEC_DEV = 16
SPANS = 4
PRE_DEV = 48
GROUPS = 16
PIECES = 4
ROWS_DEV = 64
SEQ_DEV = 20
MOST_SPAN = 28
CAP = 48
TOKENS = 1024
SLOTS = 320


def draw_residual(key, part):
    key = jax.random.fold_in(key, 11)
    column = jnp.arange(D, dtype=jnp.float32) / (D - 1.0)
    entries = jnp.clip(jax.random.normal(key, (TOKENS, D), jnp.float32), -4.0, 4.0)
    values = entries * (0.4 * jnp.power(5.0, column))[None, :]
    return values.astype(jnp.bfloat16)


def with_ends(drawn, stream_key, smallest, largest):
    place = [jax.random.randint(jax.random.fold_in(stream_key, axis), (), 0, length) for axis, length in enumerate(drawn.shape)]
    longest = drawn.shape.index(max(drawn.shape))
    neighbour = place[:longest] + [(place[longest] + 1) % drawn.shape[longest]] + place[longest + 1:]
    return drawn.at[tuple(place)].set(smallest).at[tuple(neighbour)].set(largest)


def spiked(result, key, source, target, shards_of, factor):
    owner, partner = [(jnp.arange(result.shape[axis_at]) // (result.shape[axis_at] // shards_of)).reshape([-1 if axis == axis_at else 1 for axis in range(result.ndim)]) for axis_at in (source, target)]
    chosen = jax.random.permutation(key, shards_of)[partner]
    strong = (owner == chosen) | (owner == (partner + shards_of // 2) % shards_of)
    return jnp.where(strong, factor * result, result)


def block_levels(rng, dims, cuts, least, largest):
    gain = 1.0
    for dim, shards_of in cuts:
        steps = jax.random.uniform(jax.random.fold_in(jax.random.fold_in(rng, 6), dim), (shards_of,), jnp.float32, least / len(cuts), largest / len(cuts))
        gain = gain * jnp.repeat(jnp.exp(steps), dims[dim] // shards_of).reshape((-1,) + (1,) * (len(dims) - 1 - dim))
    return gain


def split_up(count, total, most, slope):
    portions = [(1 << 20) // math.isqrt(standing ** slope) + 1 for standing in range(2, count + 1)]
    surplus, counts = total - most - (count - 1), [1] * (count - 1)
    while surplus > 0:
        candidates = [i for i in range(count - 1) if counts[i] < most]
        mass, remaining = sum([portions[i] for i in candidates]), surplus
        for i in candidates:
            extra = min(most - counts[i], max(1, remaining * portions[i] // mass), surplus)
            counts[i] = counts[i] + extra
            surplus = surplus - extra
    return np.array([most] + counts)


def ragged_sizes(key, amount, total, most, lean):
    if amount == 2:
        one = jax.random.randint(key, (), max(1, total - most), min(most, total - 1) + 1)
        return jnp.stack([one, total - one])
    tallies = jnp.asarray(split_up(amount, total, most, lean), jnp.int32)
    couples = (amount - 1) // 2
    source_of, sink = tallies[1:1 + 2 * couples:2], tallies[2:2 + 2 * couples:2]
    room = jnp.minimum(source_of - 1, most - sink)
    passed = jax.random.randint(jax.random.fold_in(key, 1), (couples,), 0, 1 << 20) % (room + 1)
    tallies = tallies.at[1:1 + 2 * couples:2].set(source_of - passed).at[2:2 + 2 * couples:2].set(sink + passed)
    return tallies[jax.random.permutation(jax.random.fold_in(key, 2), amount)]


def routed_block(stream_key, own, number, rows, count, top, most, skew):
    order = jax.random.permutation(stream_key, count)
    heavy_load, usual = portions_of(count, rows * top, most, skew, True), portions_of(count, rows * top, most, skew, False)
    places = jnp.arange(count)

    def named(sizes, turn):
        used = int((sizes > 0).sum())
        fixed = max(1, used // 4)
        moved = fixed + (places - fixed + turn * (used - fixed)) % max(1, count - fixed)
        return jnp.zeros((count,), jnp.int32).at[order[jnp.where(places < fixed, places, moved)]].set(jnp.asarray(sizes, jnp.int32))

    sizes = jnp.where(number % 4 == 0, named(heavy_load, number // 4), named(usual, number - number // 4 - 1))
    mixed = jax.random.permutation(jax.random.fold_in(own, 3), count)
    giver, receiver = mixed[0:count // 2 * 2:2], mixed[1:count // 2 * 2:2]
    room = jnp.minimum(sizes[giver] - 1, most - sizes[receiver]) // 2
    room = jnp.where((giver == order[0]) | (receiver == order[0]) | (sizes[receiver] == 0), 0, jnp.maximum(room, 0))
    moved = jax.random.randint(jax.random.fold_in(own, 4), (count // 2,), 0, 1 << 20) % (room + 1)
    sizes = sizes.at[giver].add(-moved).at[receiver].add(moved)
    members = jnp.searchsorted(jnp.cumsum(sizes), jnp.arange(rows * top), side="right").astype(jnp.int32)
    listing = members.reshape(top, rows).T
    listing = listing[jax.random.permutation(jax.random.fold_in(own, 1), rows)]
    turn = jax.random.randint(jax.random.fold_in(own, 2), (rows, 1), 0, top)
    return jnp.take_along_axis(listing, (jnp.arange(top)[None, :] + turn) % top, axis=1)


def portions_of(amount, total, limit, skew, full):
    portions = [(1 << 20) // math.isqrt(rank ** skew) + 1 for rank in range(1, amount + 1)]
    largest = limit if full else min(limit, max(-(-total // amount), total * portions[0] // sum(portions)))
    least = 1 if total - largest >= amount - 1 else 0
    given, surplus = [largest] + [least] * (amount - 1), total - largest - least * (amount - 1)
    while surplus > 0:
        candidates = [i for i in range(1, amount) if given[i] < largest] or [i for i in range(1, amount) if given[i] < limit]
        whole, left = sum([portions[i] for i in candidates]), surplus
        for i in candidates:
            addition = min(limit - given[i], max(1, left * portions[i] // whole), surplus)
            given[i] = given[i] + addition
            surplus = surplus - addition
    return np.array(given)


def bell_draw(stream_key, dims, width, most, split=(), kind=jnp.bfloat16):
    drawn = jax.random.normal(stream_key, dims, jnp.float32) * width
    if len(split) > 0:
        drawn = block_levels(stream_key, dims, split, -0.22, 0.18) * drawn
    return jnp.clip(drawn, min=-most, max=most).astype(kind)


def noise_with(own_key, extent, width, most, shards, heavy, kind=jnp.bfloat16):
    values = width * jax.random.normal(own_key, extent, jnp.float32)
    if shards:
        values = values * block_levels(own_key, extent, shards, -0.22, 0.18)
    return jnp.clip(spiked(values, jax.random.fold_in(own_key, 3), *heavy), -most, most).astype(kind)


def setup_inputs(seed: int = 0) -> dict:
    streams_of = jax.random.split(jax.random.key(seed), 25)
    conv_input = bell_draw(streams_of[0], (TOKENS, DI), 1.0, 6.0, ((0, 16), (1, 8)))
    gate_input = bell_draw(streams_of[1], (TOKENS, DI), 1.0, 6.0, ((0, 16), (1, 8)))
    conv_cache = bell_draw(streams_of[2], (SLOTS, CONV - 1, DI), 1.0, 6.0, ((0, 16), (2, 8)))
    state_cache = bell_draw(streams_of[3], (SLOTS, NS, DI), 1.0, 6.0, ((0, 16), (2, 8)), jnp.float32)
    span_lengths = jax.vmap(lambda own: ragged_sizes(own, SPANS, PRE_DEV, MOST_SPAN, 2))(jax.random.split(streams_of[4], GROUPS)).reshape((GROUPS, SPANS)).astype(jnp.int32)
    span_resumes = with_ends(jax.random.randint(streams_of[5], (GROUPS, SPANS), 0, 2), jax.random.fold_in(streams_of[5], 1), 0, 1).astype(jnp.int32)
    slot_index = jax.vmap(lambda own: jax.random.permutation(own, SEQ_DEV))(jax.random.split(streams_of[6], GROUPS)).reshape((GROUPS, SEQ_DEV)).astype(jnp.int32)
    conv_weight = bell_draw(streams_of[7], (CONV, DI), 0.5, 3.0, ((1, 8),), jnp.float32)
    conv_bias = bell_draw(streams_of[8], (DI,), 0.5, 3.0, ((0, 8),), jnp.float32)
    rank_weight = bell_draw(streams_of[9], (DI, R), DI ** -0.5, 0.0625, ((0, 8),))
    state_weight = bell_draw(streams_of[10], (DI, 2 * NS), DI ** -0.5, 0.0625, ((0, 8),))
    step_gain = jnp.clip(1.0 + 0.18 * jax.random.normal(streams_of[11], (R,), jnp.float32), 0.1, 1.9)
    step_weight = bell_draw(streams_of[12], (R, DI), R ** -0.5, 0.25, ((1, 8),))
    step_bias = jnp.clip(-6.9 + 4.6000001430511475 * jax.random.uniform(streams_of[13], (DI,), jnp.float32) ** block_levels(streams_of[13], (DI,), ((0, 8),), -0.2, 0.2), -6.9, -2.3)
    decay_log = jnp.clip(2.77 * jax.random.uniform(streams_of[14], (NS, DI), jnp.float32) ** block_levels(streams_of[14], (NS, DI), ((1, 8),), -0.2, 0.2), 0.0, 2.77)
    skip_gain = jnp.clip(0.5 + 1.0 * jax.random.uniform(streams_of[15], (DI,), jnp.float32) ** block_levels(streams_of[15], (DI,), ((0, 8),), -0.2, 0.2), 0.5, 1.5)
    out_weight = noise_with(streams_of[16], (DI, D), DI ** -0.5, 0.09375, ((0, 8),), (0, 1, 8, 2.0))
    residual = draw_residual(jax.random.fold_in(streams_of[24], 71), 0)
    moe_gain = jnp.clip(1.0 + 0.18 * jax.random.normal(streams_of[18], (D,), jnp.float32), 0.1, 1.9)
    router_weight = bell_draw(streams_of[19], (D, EXPERTS), D ** -0.5, 0.09375, ((0, 8),))
    chosen_experts_keys = jax.random.split(jax.random.fold_in(streams_of[20], 1), TOKENS // ROWS_DEV)
    chosen_experts_turns = jax.random.permutation(jax.random.fold_in(streams_of[20], 3), TOKENS // ROWS_DEV)
    chosen_experts = jax.vmap(lambda own, number: routed_block(jax.random.fold_in(streams_of[20], 2), own, number, ROWS_DEV, EXPERTS, 2, CAP, 2))(chosen_experts_keys, chosen_experts_turns).reshape((TOKENS, 2))
    gate_weight = bell_draw(streams_of[21], (EXPERTS * PIECES, D, FF // PIECES), D ** -0.5, 0.09375, ((0, 16), (2, 8)))
    up_weight = bell_draw(streams_of[22], (EXPERTS * PIECES, D, FF // PIECES), D ** -0.5, 0.09375, ((0, 16), (2, 8)))
    down_weight = noise_with(streams_of[23], (EXPERTS * PIECES, FF // PIECES, D), FF ** -0.5, 0.078125, ((0, 16), (1, 8)), (1, 2, 8, 2.0))
    return dict(conv_input=conv_input, gate_input=gate_input, conv_cache=conv_cache, state_cache=state_cache, span_lengths=span_lengths, span_resumes=span_resumes, slot_index=slot_index, conv_weight=conv_weight, conv_bias=conv_bias, rank_weight=rank_weight, state_weight=state_weight, step_gain=step_gain, step_weight=step_weight, step_bias=step_bias, decay_log=decay_log, skip_gain=skip_gain, out_weight=out_weight, residual=residual, moe_gain=moe_gain, router_weight=router_weight, chosen_experts=chosen_experts, gate_weight=gate_weight, up_weight=up_weight, down_weight=down_weight)


norm_eps = 1e-06

def row_layout(span_row, resume_row, row_count):
    lengths = jnp.concatenate([jnp.ones((DEC_DEV,), jnp.int32), span_row.astype(jnp.int32)])
    resumes = jnp.concatenate([jnp.ones((DEC_DEV,), jnp.int32), resume_row.astype(jnp.int32)])
    ends = jnp.cumsum(lengths).astype(jnp.int32)
    starts = (ends - lengths).astype(jnp.int32)
    row_number = jnp.arange(row_count, dtype=jnp.int32)
    segment = lax.optimization_barrier(jnp.sum((row_number[:, None] >= ends[None, :]).astype(jnp.int32), axis=1)).astype(jnp.int32)
    member = (segment[:, None] == jnp.arange(lengths.shape[0], dtype=jnp.int32)[None, :]).astype(jnp.int32)
    position = (row_number - lax.optimization_barrier(jnp.sum(member * starts[None, :], axis=1))).astype(jnp.int32)
    return (lengths, resumes, starts, segment, position)

def convolve(conv_input, cached_raw, resumes, segment, position, conv_weight, conv_bias):
    taps = conv_weight.shape[0]
    values = conv_input.astype(jnp.float32)
    cached = cached_raw.astype(jnp.float32) * resumes.astype(jnp.float32)[:, None, None]
    total = conv_bias[None, :] + conv_weight[taps - 1][None, :] * values
    for lag in range(1, taps):
        shifted = jnp.concatenate([jnp.zeros((lag, values.shape[1]), jnp.float32), values[:-lag]], axis=0)
        older = cached[segment, jnp.clip(taps - 1 + position - lag, 0, taps - 2)]
        total = total + conv_weight[taps - 1 - lag][None, :] * jnp.where((position >= lag)[:, None], shifted, older)
    return jax.nn.silu(total).astype(jnp.bfloat16)

def conv_tail(conv_input, cached_raw, lengths, starts, resumes, taps, row_count):
    pieces = []
    sequence = jnp.arange(lengths.shape[0], dtype=jnp.int32)
    for offset in range(taps - 1):
        back = lengths - (taps - 1) + offset
        from_rows = conv_input[jnp.clip(starts + back, 0, row_count - 1)]
        from_cache = cached_raw[sequence, jnp.clip(back + taps - 1, 0, taps - 2)]
        from_cache = jnp.where(resumes[:, None] > 0, from_cache, jnp.zeros_like(from_cache))
        pieces.append(jnp.where((back >= 0)[:, None], from_rows, from_cache))
    return jnp.stack(pieces, axis=1)

def mixer_block(conv_input, gate_input, cache_conv, cache_state, span_row, resume_row, slots, conv_weight, conv_bias, rank_weight, state_weight, step_gain, step_weight, step_bias, decay_log, skip_gain):
    row_count = conv_input.shape[0]
    taps = conv_weight.shape[0]
    slots = slots.astype(jnp.int32)
    lengths, resumes, starts, segment, position = row_layout(span_row, resume_row, row_count)
    cached_raw = cache_conv[slots]
    mixed_x = convolve(conv_input, cached_raw, resumes, segment, position, conv_weight, conv_bias)
    step_low = jnp.dot(mixed_x, rank_weight, preferred_element_type=jnp.float32)
    state_proj = jnp.dot(mixed_x, state_weight, preferred_element_type=jnp.float32)
    step_norm = (step_low * lax.rsqrt(lax.optimization_barrier(jnp.mean(step_low * step_low, axis=1, keepdims=True)) + norm_eps) * step_gain[None, :]).astype(jnp.bfloat16)
    step = jax.nn.softplus(jnp.dot(step_norm, step_weight, preferred_element_type=jnp.float32) + step_bias[None, :])
    nstate = decay_log.shape[0]
    input_b = state_proj[:, :nstate]
    output_c = state_proj[:, nstate:]
    values = mixed_x.astype(jnp.float32)
    rate = -jnp.exp(decay_log)
    initial = cache_state[slots] * resumes.astype(jnp.float32)[:, None, None]
    first = position == 0

    def advance(state, inputs):
        step_row, value_row, b_row, c_row, first_row, segment_row = inputs
        prior = jnp.where(first_row, initial[segment_row], state)
        fresh = jnp.exp(step_row[None, :] * rate) * prior + (step_row * value_row)[None, :] * b_row[:, None]
        return (fresh, (lax.optimization_barrier(jnp.sum(c_row[:, None] * fresh, axis=0)), fresh))
    zero_state = jnp.zeros(rate.shape, jnp.float32)
    last_state, (sums, states) = lax.scan(advance, zero_state, (step, values, input_b, output_c, first, segment))
    output = sums + skip_gain[None, :] * values
    gated = (output * jax.nn.silu(gate_input.astype(jnp.float32))).astype(jnp.bfloat16)
    finals = states[starts + lengths - 1]
    new_state = jnp.zeros_like(cache_state).at[slots].set(finals)
    new_conv = jnp.zeros_like(cache_conv).at[slots].set(conv_tail(conv_input, cached_raw, lengths, starts, resumes, taps, row_count))
    return (gated, new_state, new_conv)

def reference(conv_input, gate_input, conv_cache, state_cache, span_lengths, span_resumes, slot_index, conv_weight, conv_bias, rank_weight, state_weight, step_gain, step_weight, step_bias, decay_log, skip_gain, out_weight, residual, moe_gain, router_weight, chosen_experts, gate_weight, up_weight, down_weight):

    def per_group(items):
        block_x, block_z, block_conv, block_state, span_row, resume_row, slots = items
        return mixer_block(block_x, block_z, block_conv, block_state, span_row, resume_row, slots, conv_weight, conv_bias, rank_weight, state_weight, step_gain, step_weight, step_bias, decay_log, skip_gain)
    grouped = (conv_input.reshape(GROUPS, ROWS_DEV, DI), gate_input.reshape(GROUPS, ROWS_DEV, DI), conv_cache.reshape(GROUPS, SEQ_DEV, CONV - 1, DI), state_cache.reshape(GROUPS, SEQ_DEV, NS, DI), span_lengths, span_resumes, slot_index)
    gated, new_state, new_conv = lax.map(per_group, grouped)
    gated = gated.reshape(TOKENS, DI)
    new_state = new_state.reshape(SLOTS, NS, DI)
    new_conv = new_conv.reshape(SLOTS, CONV - 1, DI)
    mixer = jnp.dot(gated, out_weight, preferred_element_type=jnp.float32).astype(jnp.bfloat16)
    hidden = residual.astype(jnp.float32) + mixer.astype(jnp.float32)
    normed = (hidden * lax.rsqrt(lax.optimization_barrier(jnp.mean(hidden * hidden, axis=1, keepdims=True)) + norm_eps) * moe_gain[None, :]).astype(jnp.bfloat16)
    logits = jnp.dot(normed, router_weight, preferred_element_type=jnp.float32)
    chosen = jnp.take_along_axis(logits, chosen_experts.astype(jnp.int32), axis=1)
    route_first = jax.nn.sigmoid(chosen[:, 0] - chosen[:, 1])
    route_second = jax.nn.sigmoid(chosen[:, 1] - chosen[:, 0])
    flat_ids = chosen_experts.reshape(-1).astype(jnp.int32)
    assigned = TOKENS * 2
    bound = GROUPS * CAP

    def one_expert(expert):
        picks = jnp.nonzero(flat_ids == expert, size=bound, fill_value=assigned)[0].astype(jnp.int32)
        source = jnp.where(picks < assigned, picks // 2, 0)
        inputs = normed[source]
        total = jnp.zeros((bound, D), jnp.float32)
        for piece in range(PIECES):
            owner = PIECES * expert + piece
            gate = jnp.dot(inputs, gate_weight[owner], preferred_element_type=jnp.float32)
            upper = jnp.dot(inputs, up_weight[owner], preferred_element_type=jnp.float32)
            act = (jax.nn.silu(gate) * upper).astype(jnp.bfloat16)
            total = total + jnp.dot(act, down_weight[owner], preferred_element_type=jnp.float32)
        return (total, picks)
    outputs, picks = lax.map(one_expert, jnp.arange(EXPERTS, dtype=jnp.int32))
    placed = jnp.zeros((assigned + 1, D), jnp.float32).at[picks.reshape(-1)].set(outputs.reshape(-1, D))
    per_assign = placed[:assigned].reshape(TOKENS, 2, D)
    moe = route_first[:, None] * per_assign[:, 0] + route_second[:, None] * per_assign[:, 1]
    mixed = (hidden + moe).astype(jnp.bfloat16)
    return (mixed, new_state, new_conv)
```

```python
import functools

import jax
import jax.numpy as jnp
import numpy as np
from jax import lax
from jax.experimental import pallas as pl
from jax.experimental.pallas import tpu as pltpu
from jax.sharding import Mesh
from jax.sharding import PartitionSpec as P

DEC = 16
ROWS = 64
SEQ = 20
CAP = 48
NS = 16
TAPS = 4
EXPERTS = 4
EPS = 1e-6
BF = jnp.bfloat16
F32 = jnp.float32
I32 = jnp.int32
VMEM = pl.BlockSpec(memory_space=pltpu.VMEM)
SMEM = pl.BlockSpec(memory_space=pltpu.SMEM)
ANY = pl.BlockSpec(memory_space=pl.ANY)


def params(mib):
    return pltpu.CompilerParams(vmem_limit_bytes=mib * 1024 * 1024)


def iota(shape, dim):
    return lax.broadcasted_iota(I32, shape, dim)


def silu(v):
    return v / (1.0 + jnp.exp(-v))


def dot(a, b):
    return jnp.dot(a, b, preferred_element_type=F32)


def span_starts(span_ref):
    s1 = DEC + span_ref[0, 0]
    s2 = s1 + span_ref[0, 1]
    s3 = s2 + span_ref[0, 2]
    return (jnp.int32(DEC), s1, s2, s3)


def conv_kernel(
    span_ref, res_ref, slot_ref, x_ref, cache_ref, w_ref, b_ref, rank_ref, sw_ref,
    cx_ref, proj_ref, nc_ref, xc_ref,
):
    xc_ref[0:ROWS] = x_ref[...]
    xc_ref[ROWS : 2 * ROWS] = cache_ref[...]
    xc = xc_ref[...]
    starts = span_starts(span_ref)
    r = iota((ROWS, 128), 0)
    j = iota((ROWS, 128), 1)
    start = jnp.where(r < DEC, r, DEC)
    slot = jnp.full((ROWS, 128), slot_ref[0, DEC], I32)
    res = jnp.full((ROWS, 128), res_ref[0, 0], I32)
    for c in range(1, 4):
        inside = r >= starts[c]
        start = jnp.where(inside, starts[c], start)
        slot = jnp.where(inside, slot_ref[0, DEC + c], slot)
        res = jnp.where(inside, res_ref[0, c], res)
    for d in range(DEC):
        slot = jnp.where(r == d, slot_ref[0, d], slot)
    res = jnp.where(r < DEC, 1, res)
    pos = r - start
    total = b_ref[...] + w_ref[TAPS - 1 : TAPS] * x_ref[...].astype(F32)
    for lag in range(1, TAPS):
        older = jnp.where(res > 0, ROWS + slot * 3 + 3 + pos - lag, -1)
        pick = (j == jnp.where(pos >= lag, r - lag, older)).astype(BF)
        total = total + w_ref[TAPS - 1 - lag : TAPS - lag] * dot(pick, xc)
    cx = silu(total).astype(BF)
    cx_ref[...] = cx
    proj_ref[:, 0:512] = dot(cx, rank_ref[...]).astype(BF)
    proj_ref[:, 512:640] = jnp.zeros((ROWS, 128), BF)
    proj_ref[:, 512 : 512 + 2 * NS] = dot(cx, sw_ref[...]).astype(BF)
    group = (r * 171) >> 9
    offset = r - 3 * group
    length = jnp.ones((ROWS, 128), I32)
    first = jnp.zeros((ROWS, 128), I32)
    kept = jnp.ones((ROWS, 128), I32)
    for s in range(SEQ):
        here = group == slot_ref[0, s]
        if s < DEC:
            first = jnp.where(here, s, first)
        else:
            first = jnp.where(here, starts[s - DEC], first)
            length = jnp.where(here, span_ref[0, s - DEC], length)
            kept = jnp.where(here, res_ref[0, s - DEC], kept)
    back = length - 3 + offset
    older = jnp.where(kept > 0, ROWS + group * 3 + back + 3, -1)
    col = jnp.where(group < SEQ, jnp.where(back >= 0, first + back, older), -1)
    nc_ref[...] = dot((j == col).astype(BF), xc).astype(BF)


def scan_kernel(
    here_ref, span_ref, res_ref, slot_ref,
    q0_ref, q1_ref, q2_ref, q3_ref, cx_ref, z_ref, gain_ref, sw_ref, sb_ref, dl_ref, skip_ref,
    sc_ref, ow_ref,
    ns_ref, own_ref, sib_ref,
    w_vmem, step_ref, drive_ref, bb_ref, cb_ref, pc_ref, tr_ref, sem,
):
    fetch = pltpu.make_async_copy(ow_ref, w_vmem, sem)
    fetch.start()
    starts = span_starts(span_ref)
    proj = (
        q0_ref[...].astype(F32) + q1_ref[...].astype(F32)
        + q2_ref[...].astype(F32) + q3_ref[...].astype(F32)
    )
    low = proj[:, 0:512]
    mean = jnp.mean(low * low, axis=1, keepdims=True)
    norm = (low * lax.rsqrt(mean + EPS) * gain_ref[...]).astype(BF)
    pre = dot(norm, sw_ref[...]) + sb_ref[...]
    step = jnp.maximum(pre, 0.0) + jnp.log1p(jnp.exp(-jnp.abs(pre)))
    values = cx_ref[...].astype(F32)
    step_ref[...] = step
    drive_ref[...] = step * values
    tr_ref[0:ROWS] = proj[:, 512:640]
    tr_ref[ROWS : 2 * ROWS] = jnp.zeros((ROWS, 128), F32)
    turned = tr_ref[...].T
    for r in range(ROWS):
        bb_ref[r] = jnp.broadcast_to(turned[0:NS, r : r + 1], (NS, 128))
        cb_ref[r] = jnp.broadcast_to(turned[NS : 2 * NS, r : r + 1], (NS, 128))
    rate = -jnp.exp(dl_ref[...])
    groups = rate.shape[1] // 128

    def advance(r, state):
        c1 = (r >= starts[1]).astype(I32)
        c2 = (r >= starts[2]).astype(I32)
        c3 = (r >= starts[3]).astype(I32)
        piece = c1 + c2 + c3
        decode = r < DEC
        slot = slot_ref[0, jnp.where(decode, r, DEC + piece)]
        resumed = jnp.where(decode, 1, res_ref[0, piece])
        begins = (r <= DEC) | (r == starts[1]) | (r == starts[2]) | (r == starts[3])
        keep = jnp.where(begins, 0.0, 1.0).astype(F32)
        load = jnp.where(begins, resumed, 0).astype(F32)
        prior = state * keep + sc_ref[slot] * load
        decay = jnp.exp(step_ref[pl.ds(r, 1), :] * rate)
        b = jnp.concatenate([bb_ref[r]] * groups, axis=1)
        c = jnp.concatenate([cb_ref[r]] * groups, axis=1)
        fresh = decay * prior + drive_ref[pl.ds(r, 1), :] * b
        weighed = fresh * c
        pc_ref[r] = weighed[0:8] + weighed[8:16]
        ns_ref[slot] = fresh
        return fresh

    lax.fori_loop(0, ROWS, advance, jnp.zeros(rate.shape, F32), unroll=4)
    output = skip_ref[...] * values
    for k in range(8):
        output = output + pc_ref[:, k, :]
    gated = (output * silu(z_ref[...].astype(F32))).astype(BF)
    fetch.wait()
    x, c = here_ref[0], here_ref[1]
    for k in range(4):
        there = lax.rem(x + k, 4)
        for out, core in ((own_ref, c), (sib_ref, 1 - c)):
            cols = pl.ds(pl.multiple_of((2 * there + core) * 512, 512), 512)
            out[k] = dot(gated, w_vmem[:, cols]).astype(BF)


def pick_kernel(
    here_ref, q0_ref, q1_ref, q2_ref, q3_ref, resid_ref, gain_ref, router_ref, chosen_ref,
    hid_ref, pick_ref, stat_ref,
):
    mixer = (
        q0_ref[...].astype(F32) + q1_ref[...].astype(F32)
        + q2_ref[...].astype(F32) + q3_ref[...].astype(F32)
    ).astype(BF)
    hidden = resid_ref[...].astype(F32) + mixer.astype(F32)
    hid_ref[...] = hidden
    scaled = (hidden * gain_ref[...]).astype(BF)
    wide = scaled.astype(F32)
    lane = iota((ROWS, 128), 1)
    stat = jnp.where(lane == EXPERTS, jnp.sum(hidden * hidden, axis=1, keepdims=True), 0.0)
    for e in range(EXPERTS):
        part = jnp.sum(wide * router_ref[e : e + 1], axis=1, keepdims=True)
        stat = jnp.where(lane == e, part, stat)
    stat_ref[...] = stat
    before = (iota((ROWS, ROWS), 0) < iota((ROWS, ROWS), 1)).astype(BF)
    row = iota((CAP, ROWS), 0)
    z = here_ref[2]
    for k in range(EXPERTS):
        e = lax.rem(z + k, EXPERTS)
        marks = ((chosen_ref[0:1] == e) | (chosen_ref[1:2] == e)).astype(F32)
        marks = jnp.broadcast_to(marks, (8, ROWS))
        place = dot(marks.astype(BF), before).astype(I32)[0:1]
        hot = ((row == place) & (marks[0:1] > 0.0)).astype(BF)
        pick_ref[k] = dot(hot, scaled).astype(BF)


def gate_half(here_ref, core, x0_ref, x1_ref, gi_ref, wg_ref, wu_ref, acc_ref, sq_ref):
    x = here_ref[0]

    def step(k, carry):
        rows = pl.ds(pl.multiple_of((2 * lax.rem(x + 4 - k, 4) + core) * 512, 512), 512)
        wg, wu = wg_ref[rows, :], wu_ref[rows, :]
        inv = gi_ref[k]
        for h, block in ((0, x0_ref[:, k]), (1, x1_ref[k])):
            block = block.reshape(384, 512)
            acc_ref[h, :, 0:384] += dot(block, wg)
            acc_ref[h, :, 384:768] += dot(block, wu)
            wide = block.astype(F32)
            square = wide * wide * inv
            sq_ref[h] += square[:, 0:128] + square[:, 128:256] + square[:, 256:384] + square[:, 384:512]
        return carry

    lax.fori_loop(0, 4, step, 0)


def ffn_first(here_ref, x0_ref, x1_ref, gi_ref, wg_ref, wu_ref, acc_ref, sq_ref):
    acc_ref[...] = jnp.zeros_like(acc_ref)
    sq_ref[...] = jnp.zeros_like(sq_ref)
    gate_half(here_ref, here_ref[1], x0_ref, x1_ref, gi_ref, wg_ref, wu_ref, acc_ref, sq_ref)


def down_half(here_ref, core, act_ref, wd_ref, out0_ref, out1_ref):
    x = here_ref[0]

    def step(k, carry):
        cols = pl.ds(pl.multiple_of((2 * lax.rem(x + k, 4) + core) * 512, 512), 512)
        wd = wd_ref[:, cols]
        out0_ref[:, k] = dot(act_ref[0], wd).astype(BF).reshape(4, 96, 512)
        out1_ref[k] = dot(act_ref[1], wd).astype(BF).reshape(4, 96, 512)
        return carry

    lax.fori_loop(0, 4, step, 0)


def ffn_second(
    here_ref, x0_ref, x1_ref, gi_ref, wg_ref, wu_ref, wd_ref, acc_in, sq_in,
    act_ref, out0_ref, out1_ref, acc_ref, sq_ref,
):
    acc_ref[...] = acc_in[...]
    sq_ref[...] = sq_in[...]
    gate_half(here_ref, 1 - here_ref[1], x0_ref, x1_ref, gi_ref, wg_ref, wu_ref, acc_ref, sq_ref)
    for h in range(2):
        square = jnp.sum(sq_ref[h], axis=1, keepdims=True)
        scale = lax.rsqrt(square / 4096.0 + EPS)
        gate = acc_ref[h, :, 0:384] * scale
        act_ref[h] = (silu(gate) * (acc_ref[h, :, 384:768] * scale)).astype(BF)
    down_half(here_ref, 1 - here_ref[1], act_ref, wd_ref, out0_ref, out1_ref)


def ffn_third(here_ref, act_ref, wd_ref, out0_ref, out1_ref):
    down_half(here_ref, here_ref[1], act_ref, wd_ref, out0_ref, out1_ref)


def final_kernel(
    here_ref, r0_ref, r1_ref, r2_ref, r3_ref, s0_ref, s1_ref, s2_ref, s3_ref, hid_ref, chosen_ref,
    out_ref,
):
    stat = s0_ref[...] + s1_ref[...] + s2_ref[...] + s3_ref[...]
    scale = lax.rsqrt(stat[:, EXPERTS : EXPERTS + 1] / 4096.0 + EPS)
    e0, e1 = chosen_ref[:, 0:1], chosen_ref[:, 1:2]
    l0 = jnp.zeros((ROWS, 1), F32)
    l1 = jnp.zeros((ROWS, 1), F32)
    for e in range(EXPERTS):
        l0 = l0 + jnp.where(e0 == e, stat[:, e : e + 1], 0.0)
        l1 = l1 + jnp.where(e1 == e, stat[:, e : e + 1], 0.0)
    gap = (l0 - l1) * scale
    route0 = 1.0 / (1.0 + jnp.exp(-gap))
    route1 = 1.0 / (1.0 + jnp.exp(gap))
    before = (iota((ROWS, ROWS), 1) < iota((ROWS, ROWS), 0)).astype(BF)
    lane = iota((ROWS, CAP), 1)
    total = hid_ref[...]
    z = here_ref[2]
    for k, ret in enumerate((r0_ref, r1_ref, r2_ref, r3_ref)):
        e = lax.rem(z + k, EXPERTS)
        first, second = e0 == e, e1 == e
        marks = jnp.broadcast_to((first | second).astype(F32), (ROWS, 128))
        place = dot(before, marks.astype(BF)).astype(I32)[:, 0:CAP]
        hot = ((lane == place) & (marks[:, 0:CAP] > 0.0)).astype(BF)
        weight = jnp.where(first, route0, jnp.where(second, route1, 0.0))
        total = total + weight * dot(hot, ret[...])
    out_ref[...] = total.astype(BF)


def move(value, axis, shift):
    size = lax.axis_size(axis)
    return lax.ppermute(value, axis, [(i, (i + shift) % size) for i in range(size)])


def call(kernel, outs, ins, mib, scratch=(), flops=0, moved=0, name=None):
    single = not isinstance(outs, (list, tuple))
    return pl.pallas_call(
        kernel,
        out_shape=outs,
        in_specs=ins,
        out_specs=VMEM if single else [VMEM] * len(outs),
        scratch_shapes=list(scratch),
        compiler_params=params(mib),
        cost_estimate=pl.CostEstimate(flops=flops, bytes_accessed=moved, transcendentals=0),
        name=name,
    )


def shape(dims, dtype):
    return jax.ShapeDtypeStruct(dims, dtype)


def per_device(
    conv_input, gate_input, conv_cache, state_cache, span_lengths, span_resumes, slot_index,
    conv_weight, conv_bias, rank_weight, state_weight, step_gain, step_weight, step_bias,
    decay_log, skip_gain, out_weight, residual, moe_gain, router_weight, chosen_experts,
    gate_weight, up_weight, down_weight,
):
    here = jnp.stack(
        [lax.axis_index("x"), lax.axis_index("core"), lax.axis_index("z")]
    ).astype(I32)
    inverse = (1.0 / (moe_gain * moe_gain)).reshape(1, 512)
    inverse_sib = move(inverse, "core", 1)
    pair = jnp.concatenate([inverse, inverse_sib], axis=0)
    pairs = [pair] + [move(pair, "x", k) for k in (1, 2, 3)]
    inv_own = jnp.stack([p[0:1] for p in pairs])
    inv_sib = jnp.stack([p[1:2] for p in pairs])
    old = jnp.pad(conv_cache.reshape(SEQ * 3, 1024), ((0, 4), (0, 0)))
    cx, proj, new_conv = call(
        conv_kernel,
        [shape((ROWS, 1024), BF), shape((ROWS, 640), BF), shape((ROWS, 1024), BF)],
        [SMEM] * 3 + [VMEM] * 6,
        16,
        [pltpu.VMEM((128, 1024), BF)],
        flops=10**9,
        moved=2 * 10**6,
        name="conv",
    )(
        span_lengths, span_resumes, slot_index, conv_input, old, conv_weight,
        conv_bias.reshape(1, 1024), rank_weight, state_weight,
    )
    new_conv = new_conv[0 : SEQ * 3].reshape(SEQ, 3, 1024)
    chip = (proj.astype(F32) + move(proj, "core", 1).astype(F32)).astype(BF)
    parts = [chip] + [move(chip, "x", k) for k in (1, 2, 3)]
    new_state, own, sib = call(
        scan_kernel,
        [
            shape((SEQ, NS, 1024), F32),
            shape((4, ROWS, 512), BF),
            shape((4, ROWS, 512), BF),
        ],
        [SMEM] * 4 + [VMEM] * 12 + [ANY],
        32,
        [
            pltpu.VMEM((1024, 4096), BF),
            pltpu.VMEM((ROWS, 1024), F32),
            pltpu.VMEM((ROWS, 1024), F32),
            pltpu.VMEM((ROWS, NS, 128), F32),
            pltpu.VMEM((ROWS, NS, 128), F32),
            pltpu.VMEM((ROWS, 8, 1024), F32),
            pltpu.VMEM((128, 128), F32),
            pltpu.SemaphoreType.DMA,
        ],
        flops=10**9,
        moved=10**7,
        name="scan",
    )(
        here, span_lengths, span_resumes, slot_index, *parts, cx, gate_input,
        step_gain.reshape(1, 512), step_weight, step_bias.reshape(1, 1024), decay_log,
        skip_gain.reshape(1, 1024), state_cache, out_weight,
    )
    mixed = (own.astype(F32) + move(sib, "core", 1).astype(F32)).astype(BF)
    parts = [mixed[0]] + [move(mixed[k], "x", k) for k in (1, 2, 3)]
    hidden, picks, stat = call(
        pick_kernel,
        [shape((ROWS, 512), F32), shape((4, CAP, 512), BF), shape((ROWS, 128), F32)],
        [SMEM] + [VMEM] * 8,
        8,
        flops=10**8,
        moved=10**6,
        name="pick",
    )(
        here, *parts, residual, moe_gain.reshape(1, 512), router_weight.astype(F32).T,
        chosen_experts.T,
    )
    rows = [picks[0]] + [move(picks[k], "z", k) for k in (1, 2, 3)]
    half0 = jnp.concatenate(rows[0:2], axis=0)
    half1 = jnp.concatenate(rows[2:4], axis=0)
    half0 = jnp.stack([half0] + [move(half0, "x", k) for k in (1, 2, 3)])
    half1 = jnp.stack([half1] + [move(half1, "y", k) for k in (1, 2, 3)])
    stat = stat + move(stat, "core", 1)
    stats = [stat] + [move(stat, "x", k) for k in (1, 2, 3)]
    half0 = jnp.stack([half0] + [move(half0, "y", k) for k in (1, 2, 3)])
    half1 = jnp.stack([half1] + [move(half1, "x", k) for k in (1, 2, 3)])
    sib0, sib1 = move(half0, "core", 1), move(half1, "core", 1)
    acc, square = call(
        ffn_first,
        [shape((2, 384, 768), F32), shape((2, 384, 128), F32)],
        [SMEM] + [VMEM] * 5,
        28,
        flops=2 * 768 * 2048 * 768,
        moved=6 * 10**6,
        name="gate_own",
    )(here, half0, half1, inv_own, gate_weight[0], up_weight[0])
    act, sib0, sib1 = call(
        ffn_second,
        [shape((2, 384, 384), BF), shape((4, 4, 96, 512), BF), shape((4, 4, 96, 512), BF)],
        [SMEM] + [VMEM] * 8,
        40,
        [pltpu.VMEM((2, 384, 768), F32), pltpu.VMEM((2, 384, 128), F32)],
        flops=3 * 768 * 2048 * 768,
        moved=8 * 10**6,
        name="gate_sib",
    )(
        here, sib0, sib1, inv_sib, gate_weight[0], up_weight[0], down_weight[0], acc, square
    )
    own0, own1 = call(
        ffn_third,
        [shape((4, 4, 96, 512), BF), shape((4, 4, 96, 512), BF)],
        [SMEM] + [VMEM] * 2,
        24,
        flops=768 * 2048 * 768,
        moved=4 * 10**6,
        name="down_own",
    )(here, act, down_weight[0])
    back0, back1 = move(sib0, "core", 1), move(sib1, "core", 1)

    def join(values):
        total = values[0].astype(F32)
        for value in values[1:]:
            total = total + value.astype(F32)
        return total.astype(BF)

    back0 = join([own0, back0])
    back1 = join([own1, back1])
    back0 = join([back0[0]] + [move(back0[j], "y", 4 - j) for j in (1, 2, 3)])
    back1 = join([back1[0]] + [move(back1[k], "x", k) for k in (1, 2, 3)])
    back0 = join([back0[0]] + [move(back0[k], "x", k) for k in (1, 2, 3)])
    back1 = join([back1[0]] + [move(back1[j], "y", 4 - j) for j in (1, 2, 3)])
    returned = [back0[0:CAP], back0[CAP : 2 * CAP], back1[0:CAP], back1[CAP : 2 * CAP]]
    returned = [returned[0]] + [move(returned[k], "z", 4 - k) for k in (1, 2, 3)]
    out = call(
        final_kernel,
        shape((ROWS, 512), BF),
        [SMEM] + [VMEM] * 10,
        8,
        flops=10**8,
        moved=10**6,
        name="combine",
    )(here, *returned, *stats, hidden, chosen_experts)
    return (out, new_state, new_conv)


def solution(mesh):
    grid = Mesh(mesh.devices.reshape(4, 4, 4, 2), ("z", "y", "x", "core"))
    group, tensor = ("z", "y"), ("x", "core")
    return jax.shard_map(
        per_device,
        mesh=grid,
        in_specs=(
            P(group, tensor),
            P(group, tensor),
            P(group, None, tensor),
            P(group, None, tensor),
            P(group, None),
            P(group, None),
            P(group, None),
            P(None, tensor),
            P(tensor),
            P(tensor, None),
            P(tensor, None),
            P(),
            P(None, tensor),
            P(tensor),
            P(None, tensor),
            P(tensor),
            P(tensor, None),
            P(group, tensor),
            P(tensor),
            P(tensor, None),
            P(group, None),
            P(group, None, tensor),
            P(group, None, tensor),
            P(group, tensor, None),
        ),
        out_specs=(P(group, tensor), P(group, None, tensor), P(group, None, tensor)),
        check_vma=False,
    )
```

```python
import functools

import jax
import jax.numpy as jnp
import numpy as np
from jax import lax
from jax.experimental import pallas as pl
from jax.experimental.pallas import tpu as pltpu
from jax.sharding import Mesh
from jax.sharding import PartitionSpec as P

DEC = 16
ROWS = 64
SEQ = 20
CAP = 48
NS = 16
TAPS = 4
EXPERTS = 4
EPS = 1e-6
BF = jnp.bfloat16
F32 = jnp.float32
I32 = jnp.int32
VMEM = pl.BlockSpec(memory_space=pltpu.VMEM)
SMEM = pl.BlockSpec(memory_space=pltpu.SMEM)
HBM = pl.BlockSpec(memory_space=pltpu.HBM)
AXES = ("z", "y", "x", "core")


def params(mib):
    return pltpu.CompilerParams(vmem_limit_bytes=mib * 1024 * 1024)


def iota(shape, dim):
    return lax.broadcasted_iota(I32, shape, dim)


def silu(v):
    return v / (1.0 + jnp.exp(-v))


def dot(a, b):
    return jnp.dot(a, b, preferred_element_type=F32)


def span_starts(span_ref):
    s1 = DEC + span_ref[0, 0]
    s2 = s1 + span_ref[0, 1]
    s3 = s2 + span_ref[0, 2]
    return (jnp.int32(DEC), s1, s2, s3)


def conv_kernel(
    span_hbm, res_hbm, slot_hbm, x_hbm, cache_hbm, w_hbm, b_hbm, rank_hbm, sw_hbm, gain_hbm,
    cx_ref, proj_ref, nc_ref,
    span_ref, res_ref, slot_ref, x_ref, cache_ref, w_ref, b_ref, rank_ref, sw_ref, gain_ref, sems,
):
    sources = (span_hbm, res_hbm, slot_hbm, x_hbm, cache_hbm, w_hbm, b_hbm, gain_hbm, sw_hbm, rank_hbm)
    targets = (span_ref, res_ref, slot_ref, x_ref, cache_ref, w_ref, b_ref, gain_ref, sw_ref, rank_ref)
    copies = [
        pltpu.make_async_copy(source, target, sems.at[i])
        for i, (source, target) in enumerate(zip(sources, targets))
    ]
    for copy in copies:
        copy.start()
    for copy in copies[:7]:
        copy.wait()
    starts = span_starts(span_ref)
    x = x_ref[...]
    r = iota((ROWS, 128), 0)
    j = iota((ROWS, 128), 1)
    start = jnp.where(r < DEC, r, DEC)
    slot = jnp.full((ROWS, 128), slot_ref[0, DEC], I32)
    res = jnp.full((ROWS, 128), res_ref[0, 0], I32)
    for c in range(1, 4):
        inside = r >= starts[c]
        start = jnp.where(inside, starts[c], start)
        slot = jnp.where(inside, slot_ref[0, DEC + c], slot)
        res = jnp.where(inside, res_ref[0, c], res)
    for d in range(DEC):
        slot = jnp.where(r == d, slot_ref[0, d], slot)
    res = jnp.where(r < DEC, 1, res)
    pos = r - start

    def select(column, line, width):
        return (j == jnp.where(line, column, -1)).astype(F32)[:, 0:width].astype(BF)

    total = b_ref[...] + w_ref[TAPS - 1 : TAPS] * x.astype(F32)
    for lag in range(1, TAPS):
        value = dot(select(r - lag, pos >= lag, ROWS), x)
        for i in range(TAPS - 1):
            old = (pos == i + lag - 3) & (pos < lag) & (res > 0)
            value = value + dot(select(slot, old, SEQ), cache_ref[i])
        total = total + w_ref[TAPS - 1 - lag : TAPS - lag] * value
    cx = silu(total).astype(BF)
    cx_ref[...] = cx
    for copy in copies[7:]:
        copy.wait()
    proj_ref[0:ROWS, 0:512] = dot(cx, rank_ref[...]).astype(BF)
    proj_ref[0:ROWS, 512:640] = jnp.zeros((ROWS, 128), BF)
    proj_ref[0:ROWS, 512 : 512 + 2 * NS] = lax.dot_general(
        cx, sw_ref[...], (((1,), (1,)), ((), ())), preferred_element_type=F32
    ).astype(BF)
    line = 2 * (2 * lax.axis_index("x") + lax.axis_index("core"))
    inverse = 1.0 / (gain_ref[...] * gain_ref[...])
    high = inverse.astype(BF).astype(F32)
    row = iota((16, 512), 0)
    extra = jnp.where(row == line, high, jnp.where(row == line + 1, inverse - high, 0.0))
    proj_ref[ROWS : ROWS + 16, 0:512] = extra.astype(BF)
    proj_ref[ROWS : ROWS + 16, 512:640] = jnp.zeros((16, 128), BF)
    group = r
    length = jnp.ones((ROWS, 128), I32)
    first = jnp.zeros((ROWS, 128), I32)
    kept = jnp.ones((ROWS, 128), I32)
    for s in range(SEQ):
        here = group == slot_ref[0, s]
        if s < DEC:
            first = jnp.where(here, s, first)
        else:
            first = jnp.where(here, starts[s - DEC], first)
            length = jnp.where(here, span_ref[0, s - DEC], length)
            kept = jnp.where(here, res_ref[0, s - DEC], kept)
    for offset in range(TAPS - 1):
        back = length - (TAPS - 1) + offset
        value = dot(select(first + back, back >= 0, ROWS), x)
        for i in range(TAPS - 1):
            old = (back == i - 3) & (kept > 0)
            value = value + dot(select(group, old, SEQ), cache_ref[i])
        nc_ref[offset] = value[0:SEQ].astype(BF)


def scan_kernel(
    here_ref, span_ref, res_ref, slot_ref,
    q0_ref, q1_ref, q2_ref, q3_ref, cx_ref, z_ref, gain_ref, sw_ref, sb_ref, dl_ref, skip_ref,
    sc_ref, ow_ref,
    ns_ref, own_ref, sib_ref, inv_ref,
    w_vmem, step_ref, drive_ref, bb_ref, cb_ref, pc_ref, tr_ref, sem,
):
    fetch = pltpu.make_async_copy(ow_ref, w_vmem, sem)
    fetch.start()
    starts = span_starts(span_ref)
    sums = (
        q0_ref[...].astype(F32) + q1_ref[...].astype(F32)
        + q2_ref[...].astype(F32) + q3_ref[...].astype(F32)
    )
    proj = sums[0:ROWS]
    for t in range(8):
        inverse = sums[ROWS + 2 * t : ROWS + 2 * t + 1, 0:512] + sums[ROWS + 2 * t + 1 : ROWS + 2 * t + 2, 0:512]
        inv_ref[t // 2, :, 512 * (t % 2) : 512 * (t % 2) + 512] = inverse
    low = proj[:, 0:512]
    mean = jnp.mean(low * low, axis=1, keepdims=True)
    norm = (low * lax.rsqrt(mean + EPS) * gain_ref[...]).astype(BF)
    pre = dot(norm, sw_ref[...]) + sb_ref[...]
    step = jnp.maximum(pre, 0.0) + jnp.log1p(jnp.exp(-jnp.abs(pre)))
    values = cx_ref[...].astype(F32)
    step_ref[...] = step
    drive_ref[...] = step * values
    tr_ref[0:ROWS] = proj[:, 512:640]
    tr_ref[ROWS : 2 * ROWS] = jnp.zeros((ROWS, 128), F32)
    turned = tr_ref[...].T
    for r in range(ROWS):
        bb_ref[r] = jnp.broadcast_to(turned[0:NS, r : r + 1], (NS, 128))
        cb_ref[r] = jnp.broadcast_to(turned[NS : 2 * NS, r : r + 1], (NS, 128))
    rate = -jnp.exp(dl_ref[...])
    groups = rate.shape[1] // 128

    def advance(r, state):
        c1 = (r >= starts[1]).astype(I32)
        c2 = (r >= starts[2]).astype(I32)
        c3 = (r >= starts[3]).astype(I32)
        piece = c1 + c2 + c3
        decode = r < DEC
        slot = slot_ref[0, jnp.where(decode, r, DEC + piece)]
        resumed = jnp.where(decode, 1, res_ref[0, piece])
        begins = (r <= DEC) | (r == starts[1]) | (r == starts[2]) | (r == starts[3])
        keep = jnp.where(begins, 0.0, 1.0).astype(F32)
        load = jnp.where(begins, resumed, 0).astype(F32)
        prior = state * keep + sc_ref[slot] * load
        decay = jnp.exp(step_ref[pl.ds(r, 1), :] * rate)
        b = jnp.concatenate([bb_ref[r]] * groups, axis=1)
        c = jnp.concatenate([cb_ref[r]] * groups, axis=1)
        fresh = decay * prior + drive_ref[pl.ds(r, 1), :] * b
        weighed = fresh * c
        pc_ref[r] = weighed[0:8] + weighed[8:16]
        ns_ref[slot] = fresh
        return fresh

    lax.fori_loop(0, ROWS, advance, jnp.zeros(rate.shape, F32), unroll=4)
    output = skip_ref[...] * values
    for k in range(8):
        output = output + pc_ref[:, k, :]
    gated = (output * silu(z_ref[...].astype(F32))).astype(BF)
    fetch.wait()
    x, c = here_ref[0], here_ref[1]
    for out, core in ((own_ref, c), (sib_ref, 1 - c)):
        for k in range(4):
            cols = pl.ds(pl.multiple_of((2 * lax.rem(x + k, 4) + core) * 512, 512), 512)
            out[k] = dot(gated, w_vmem[:, cols]).astype(BF)


def pick_kernel(
    here_ref, q0_ref, q1_ref, q2_ref, q3_ref, resid_ref, gain_ref, router_ref, chosen_ref,
    hid_ref, mine_ref, theirs_ref, named_ref,
):
    mixer = (
        q0_ref[...].astype(F32) + q1_ref[...].astype(F32)
        + q2_ref[...].astype(F32) + q3_ref[...].astype(F32)
    ).astype(BF)
    hidden = resid_ref[...].astype(F32) + mixer.astype(F32)
    hid_ref[...] = hidden
    scaled = (hidden * gain_ref[...]).astype(BF)
    wide = scaled.astype(F32)
    lane = iota((ROWS, 128), 1)
    squares = jnp.sum(hidden * hidden, axis=1, keepdims=True)
    stat = jnp.where(lane % 64 == EXPERTS, squares, 0.0)
    for e in range(EXPERTS):
        part = jnp.sum(wide * router_ref[e : e + 1].astype(F32), axis=1, keepdims=True)
        stat = jnp.where(lane % 64 == e, part, stat)
    high = stat.astype(BF).astype(F32)
    stat = jnp.where(lane < 64, high, stat - high).astype(BF)
    for out in (mine_ref, theirs_ref):
        out[0, :, 512:640] = stat[0:CAP]
        out[1, :, 512:640] = jnp.concatenate([stat[CAP:ROWS], jnp.zeros((2 * CAP - ROWS, 128), BF)], axis=0)
    before = (iota((ROWS, ROWS), 0) < iota((ROWS, ROWS), 1)).astype(F32).astype(BF)
    row = iota((CAP, ROWS), 0)
    z, core = here_ref[2], here_ref[1]
    for out, side in ((mine_ref, core), (theirs_ref, 1 - core)):
        for i in range(2):
            e = lax.rem(z + 2 * side + i, EXPERTS)
            marks = ((chosen_ref[0:1] == e) | (chosen_ref[1:2] == e)).astype(F32)
            marks = jnp.broadcast_to(marks, (8, ROWS))
            place = dot(marks.astype(BF), before).astype(I32)[0:1]
            hot = ((row == place) & (marks[0:1] > 0.0)).astype(F32).astype(BF)
            out[i, :, 0:512] = dot(hot, scaled).astype(BF)
    same = (iota((ROWS, ROWS), 0) == iota((ROWS, ROWS), 1)).astype(F32).astype(BF)
    pair = iota((8, ROWS), 0)
    both = jnp.where(pair == 0, chosen_ref[0:1], jnp.where(pair == 1, chosen_ref[1:2], 0))
    turned = lax.dot_general(
        same, both.astype(F32).astype(BF), (((1,), (1,)), ((), ())), preferred_element_type=F32
    )
    named_ref[...] = jnp.zeros_like(named_ref)
    named_ref[:, 0:8] = turned.astype(I32)


def experts_in(here_ref, side, x_ref, inv_ref, wg_ref, wu_ref):
    x = here_ref[0]
    by_row, by_col = jnp.where(side == 0, 4, 1), jnp.where(side == 0, 1, 4)
    gate = upper = square = None
    for k in range(4):
        there = lax.rem(x + 4 - k, 4)
        rows = pl.ds(pl.multiple_of(there * 1024, 1024), 1024)
        block = jnp.concatenate([x_ref[j * by_row + k * by_col] for j in range(4)], axis=0)
        gate_part = dot(block, wg_ref[rows, :])
        upper_part = dot(block, wu_ref[rows, :])
        wide = block.astype(F32)
        wide = wide * wide * inv_ref[there]
        square_part = wide[:, 0:128]
        for lane in range(128, 1024, 128):
            square_part = square_part + wide[:, lane : lane + 128]
        if k == 0:
            gate, upper, square = gate_part, upper_part, square_part
        else:
            gate, upper, square = gate + gate_part, upper + upper_part, square + square_part
    scale = lax.rsqrt(jnp.sum(square, axis=1, keepdims=True) / 4096.0 + EPS)
    return (silu(gate * scale) * (upper * scale)).astype(BF)


def experts_out(here_ref, side, act_ref, wd_ref, outs):
    x = here_ref[0]

    def product(k):
        cols = pl.ds(pl.multiple_of(lax.rem(x + k, 4) * 1024, 1024), 1024)
        return dot(act_ref[...], wd_ref[:, cols]).astype(BF)

    @pl.when(side == 0)
    def _():
        for k in range(4):
            value = product(k)
            for j in range(4):
                outs[(4 - j) % 4][k] = value[96 * j : 96 * j + 96]

    @pl.when(side == 1)
    def _():
        for k in range(4):
            value = product(k)
            for j in range(4):
                outs[k][(4 - j) % 4] = value[96 * j : 96 * j + 96]


def ffn_first(here_ref, x_ref, inv_ref, wg_ref, wu_ref, act_ref):
    act_ref[...] = experts_in(here_ref, here_ref[1], x_ref, inv_ref, wg_ref, wu_ref)


def ffn_second(
    here_ref, x_ref, inv_ref, wg_ref, wu_ref, wd_ref, earlier_ref,
    p0_ref, p1_ref, p2_ref, p3_ref, act_ref,
):
    side = 1 - here_ref[1]
    act_ref[...] = experts_in(here_ref, side, x_ref, inv_ref, wg_ref, wu_ref)
    experts_out(here_ref, side, act_ref, wd_ref, (p0_ref, p1_ref, p2_ref, p3_ref))


def ffn_third(here_ref, act_ref, wd_ref, p0_ref, p1_ref, p2_ref, p3_ref):
    experts_out(here_ref, here_ref[1], act_ref, wd_ref, (p0_ref, p1_ref, p2_ref, p3_ref))


def final_kernel(
    here_ref, mine_ref, theirs_ref, stat_ref, hid_ref, chosen_ref, out_ref,
):
    stat = stat_ref[0:ROWS].astype(F32)

    def column(e):
        return stat[:, e : e + 1] + stat[:, 64 + e : 65 + e]

    scale = lax.rsqrt(column(EXPERTS) / 4096.0 + EPS)
    e0, e1 = chosen_ref[:, 0:1], chosen_ref[:, 1:2]
    l0 = jnp.zeros((ROWS, 1), F32)
    l1 = jnp.zeros((ROWS, 1), F32)
    for e in range(EXPERTS):
        l0 = l0 + jnp.where(e0 == e, column(e), 0.0)
        l1 = l1 + jnp.where(e1 == e, column(e), 0.0)
    gap = (l0 - l1) * scale
    route0 = 1.0 / (1.0 + jnp.exp(-gap))
    route1 = 1.0 / (1.0 + jnp.exp(gap))
    before = (iota((ROWS, ROWS), 1) < iota((ROWS, ROWS), 0)).astype(F32).astype(BF)
    lane = iota((ROWS, CAP), 1)
    total = hid_ref[...]
    z, core = here_ref[2], here_ref[1]
    for ref, side in ((mine_ref, core), (theirs_ref, 1 - core)):
        for i in range(2):
            e = lax.rem(z + 2 * side + i, EXPERTS)
            first, second = e0 == e, e1 == e
            marks = jnp.broadcast_to((first | second).astype(F32), (ROWS, 128))
            place = dot(before, marks.astype(BF)).astype(I32)[:, 0:CAP]
            hot = ((lane == place) & (marks[:, 0:CAP] > 0.0)).astype(F32).astype(BF)
            weight = jnp.where(first, route0, jnp.where(second, route1, 0.0))
            total = total + weight * dot(hot, ref[i])
    out_ref[...] = total.astype(BF)


def move(value, axis, shift):
    size = lax.axis_size(axis)
    return lax.ppermute(value, axis, [(i, (i + shift) % size) for i in range(size)])


def by_core(value, first, second):
    sizes = tuple(lax.axis_size(name) for name in AXES)
    pairs = []
    for source in range(int(np.prod(sizes))):
        place = list(np.unravel_index(source, sizes))
        axis, shift = (first, second)[int(place[3])]
        at = AXES.index(axis)
        place[at] = (place[at] + shift) % sizes[at]
        pairs.append((source, int(np.ravel_multi_index(place, sizes))))
    return lax.ppermute(value, AXES, pairs)


def across(value, shift):
    return by_core(value, ("x", shift), ("y", shift))


def along(value, shift):
    return by_core(value, ("y", shift), ("x", shift))


def summed(*values):
    total = values[0].astype(F32)
    for value in values[1:]:
        total = total + value.astype(F32)
    return total[..., 0:64] + total[..., 64:128]


def coded(value):
    high = value.astype(BF)
    low = (value - high.astype(F32)).astype(BF)
    return jnp.concatenate([high, low], axis=-1)


def add(*values):
    total = values[0].astype(F32)
    for value in values[1:]:
        total = total + value.astype(F32)
    return total.astype(BF)


def stay(value):
    return pltpu.with_memory_space_constraint(value, pltpu.HBM)


def call(kernel, outs, ins, mib, scratch=(), flops=0, moved=0, name=None):
    single = not isinstance(outs, (list, tuple))
    return pl.pallas_call(
        kernel,
        out_shape=outs,
        in_specs=ins,
        out_specs=VMEM if single else [VMEM] * len(outs),
        scratch_shapes=list(scratch),
        compiler_params=params(mib),
        cost_estimate=pl.CostEstimate(flops=flops, bytes_accessed=moved, transcendentals=0),
        name=name,
    )


def shape(dims, dtype):
    return jax.ShapeDtypeStruct(dims, dtype)


def per_device(
    conv_input, gate_input, conv_cache, state_cache, span_lengths, span_resumes, slot_index,
    conv_weight, conv_bias, rank_weight, state_weight, step_gain, step_weight, step_bias,
    decay_log, skip_gain, out_weight, residual, moe_gain, router_weight, chosen_experts,
    gate_weight, up_weight, down_weight,
):
    here = jnp.stack(
        [lax.axis_index("x"), lax.axis_index("core"), lax.axis_index("z")]
    ).astype(I32)
    even = lax.axis_index("core") == 0
    cx, proj, new_conv = call(
        conv_kernel,
        [shape((ROWS, 1024), BF), shape((ROWS + 16, 640), BF), shape((3, SEQ, 1024), BF)],
        [HBM] * 10,
        16,
        [
            pltpu.SMEM((1, 4), I32),
            pltpu.SMEM((1, 4), I32),
            pltpu.SMEM((1, SEQ), I32),
            pltpu.VMEM((ROWS, 1024), BF),
            pltpu.VMEM((3, SEQ, 1024), BF),
            pltpu.VMEM((TAPS, 1024), F32),
            pltpu.VMEM((1, 1024), F32),
            pltpu.VMEM((1024, 512), BF),
            pltpu.VMEM((2 * NS, 1024), BF),
            pltpu.VMEM((1, 512), F32),
            pltpu.SemaphoreType.DMA((10,)),
        ],
        flops=10**9,
        moved=2 * 10**6,
        name="conv",
    )(
        *map(
            stay,
            (
                span_lengths, span_resumes, slot_index, conv_input,
                conv_cache.transpose(1, 0, 2), conv_weight, conv_bias.reshape(1, 1024),
                rank_weight, state_weight.T, moe_gain.reshape(1, 512),
            ),
        )
    )
    chip = add(proj, move(proj, "core", 1))
    parts = [chip] + [move(chip, "x", k) for k in (1, 2, 3)]
    new_state, own, sib, inverse = call(
        scan_kernel,
        [
            shape((SEQ, NS, 1024), F32),
            shape((4, ROWS, 512), BF),
            shape((4, ROWS, 512), BF),
            shape((4, 1, 1024), F32),
        ],
        [SMEM] * 4 + [VMEM] * 12 + [HBM],
        32,
        [
            pltpu.VMEM((1024, 4096), BF),
            pltpu.VMEM((ROWS, 1024), F32),
            pltpu.VMEM((ROWS, 1024), F32),
            pltpu.VMEM((ROWS, NS, 128), F32),
            pltpu.VMEM((ROWS, NS, 128), F32),
            pltpu.VMEM((ROWS, 8, 1024), F32),
            pltpu.VMEM((128, 128), F32),
            pltpu.SemaphoreType.DMA,
        ],
        flops=10**9,
        moved=10**7,
        name="scan",
    )(
        here, span_lengths, span_resumes, slot_index, *parts, cx, gate_input,
        step_gain.reshape(1, 512), step_weight, step_bias.reshape(1, 1024), decay_log,
        skip_gain.reshape(1, 1024), state_cache, stay(out_weight),
    )
    mixed = add(own, move(sib, "core", 1))
    parts = [mixed[0]] + [move(mixed[k], "x", k) for k in (1, 2, 3)]
    hidden, mine, theirs, named = call(
        pick_kernel,
        [
            shape((ROWS, 512), F32),
            shape((2, CAP, 640), BF),
            shape((2, CAP, 640), BF),
            shape((ROWS, 128), I32),
        ],
        [SMEM] + [VMEM] * 8,
        8,
        flops=10**8,
        moved=10**6,
        name="pick",
    )(here, *parts, residual, moe_gain.reshape(1, 512), router_weight.T, chosen_experts.T)
    theirs = move(theirs, "core", 1)
    stat = coded(summed(mine[:, :, 512:640], theirs[:, :, 512:640])).reshape(2 * CAP, 128)
    mine, theirs = mine[:, :, 0:512], theirs[:, :, 0:512]
    rows = jnp.concatenate([jnp.where(even, mine, theirs), jnp.where(even, theirs, mine)], axis=2)
    later = by_core(rows[1], ("z", 1), ("z", 3))
    sooner = by_core(rows[0], ("z", 0), ("z", 2))
    rows = jnp.concatenate([jnp.concatenate([sooner, later], axis=0), stat], axis=1)
    rows1, rows3 = across(rows, 1), across(rows, 3)
    rows2 = jnp.concatenate([across(rows1[0:CAP], 1), across(rows3[CAP : 2 * CAP], 3)], axis=0)

    stat = coded(summed(*[part[:, 1024:1152] for part in (rows, rows1, rows2, rows3)]))
    upper = jnp.stack([rows[:, 0:1024], rows1[:, 0:1024]])
    lower = jnp.stack([rows2[:, 0:1024], rows3[:, 0:1024]])
    upper1, lower3 = along(upper, 1), along(lower, 3)
    lower1, upper3 = along(lower, 1), along(upper, 3)
    upper2, lower2 = along(upper1, 1), along(lower3, 3)
    mine = jnp.concatenate(
        [upper, lower, upper1, lower1, upper2, lower2, upper3, lower3], axis=0
    )
    theirs = move(mine, "core", 1)
    gate, up, down = gate_weight[0], up_weight[0], down_weight[0]
    act = call(
        ffn_first,
        shape((384, 384), BF),
        [SMEM] + [VMEM] * 4,
        24,
        flops=2 * 384 * 4096 * 768,
        moved=10 * 10**6,
        name="experts_in",
    )(here, mine, inverse, gate, up)
    blocks = [shape((4, 96, 1024), BF)] * 4
    theirs = call(
        ffn_second,
        blocks,
        [SMEM] + [VMEM] * 6,
        32,
        [pltpu.VMEM((384, 384), BF)],
        flops=3 * 384 * 4096 * 768,
        moved=12 * 10**6,
        name="experts_other",
    )(here, theirs, inverse, gate, up, down, act)
    mine = call(
        ffn_third,
        blocks,
        [SMEM] + [VMEM] * 2,
        20,
        flops=384 * 4096 * 768,
        moved=6 * 10**6,
        name="experts_out",
    )(here, act, down)
    part = [None] * 4
    for m in (2, 1, 3, 0):
        part[m] = add(mine[m], move(theirs[m], "core", 1))
    far1, far3 = along(part[2][0:2], 1), along(part[2][2:4], 3)
    near1, near3 = along(part[1][2:4], 1), along(part[3][0:2], 3)
    next1, next3 = along(add(part[1][0:2], far1), 1), along(add(part[3][2:4], far3), 3)
    lines = jnp.concatenate(
        [add(part[0][0:2], next1, near3), add(part[0][2:4], near1, next3)], axis=0
    )
    lines = add(lines[0], *[across(lines[k], k) for k in (1, 2, 3)])
    later = by_core(lines[CAP : 2 * CAP], ("z", 3), ("z", 1))
    sooner = by_core(lines[0:CAP], ("z", 0), ("z", 2))
    lines = jnp.stack([sooner, later])
    left, right = lines[:, :, 0:512], lines[:, :, 512:1024]
    mine = jnp.where(even, left, right)
    theirs = jnp.concatenate([jnp.where(even, right, left), stat.reshape(2, CAP, 128)], axis=2)
    theirs = move(theirs, "core", 1)
    stat = jnp.where(even, stat, theirs[:, :, 512:640].reshape(2 * CAP, 128))
    theirs = theirs[:, :, 0:512]
    out = call(
        final_kernel,
        shape((ROWS, 512), BF),
        [SMEM] + [VMEM] * 5,
        8,
        flops=10**8,
        moved=10**6,
        name="combine",
    )(here, mine, theirs, stat, hidden, named)
    new_conv = new_conv.transpose(1, 0, 2)
    return (out, new_state, new_conv)


def solution(mesh):
    grid = Mesh(mesh.devices.reshape(4, 4, 4, 2), AXES)
    group, tensor = ("z", "y"), ("x", "core")
    return jax.shard_map(
        per_device,
        mesh=grid,
        in_specs=(
            P(group, tensor),
            P(group, tensor),
            P(group, None, tensor),
            P(group, None, tensor),
            P(group, None),
            P(group, None),
            P(group, None),
            P(None, tensor),
            P(tensor),
            P(tensor, None),
            P(tensor, None),
            P(),
            P(None, tensor),
            P(tensor),
            P(None, tensor),
            P(tensor),
            P(tensor, None),
            P(group, tensor),
            P(tensor),
            P(tensor, None),
            P(group, None),
            P(group, None, tensor),
            P(group, None, tensor),
            P(group, tensor, None),
        ),
        out_specs=(P(group, tensor), P(group, None, tensor), P(group, None, tensor)),
        check_vma=False,
    )
```

```python
import functools

import jax
import jax.numpy as jnp
import numpy as np
from jax import lax
from jax.experimental import pallas as pl
from jax.experimental.pallas import tpu as pltpu
from jax.sharding import Mesh
from jax.sharding import PartitionSpec as P

DEC = 16
ROWS = 64
SEQ = 20
CAP = 48
NS = 16
TAPS = 4
EXPERTS = 4
EPS = 1e-6
BF = jnp.bfloat16
F32 = jnp.float32
I32 = jnp.int32
VMEM = pl.BlockSpec(memory_space=pltpu.VMEM)
SMEM = pl.BlockSpec(memory_space=pltpu.SMEM)
HBM = pl.BlockSpec(memory_space=pltpu.HBM)
AXES = ("z", "y", "x", "core")


def params(mib):
    return pltpu.CompilerParams(vmem_limit_bytes=mib * 1024 * 1024)


def iota(shape, dim):
    return lax.broadcasted_iota(I32, shape, dim)


def silu(v):
    return v / (1.0 + jnp.exp(-v))


def dot(a, b):
    return jnp.dot(a, b, preferred_element_type=F32)


def span_starts(span_ref):
    s1 = DEC + span_ref[0, 0]
    s2 = s1 + span_ref[0, 1]
    s3 = s2 + span_ref[0, 2]
    return (jnp.int32(DEC), s1, s2, s3)


def conv_kernel(
    span_hbm, res_hbm, slot_hbm, x_hbm, cache_hbm, w_hbm, b_hbm, rank_hbm, sw_hbm, gain_hbm,
    cx_ref, proj_ref,
    span_ref, res_ref, slot_ref, x_ref, cache_ref, w_ref, b_ref, rank_ref, sw_ref, gain_ref, sems,
):
    sources = (span_hbm, res_hbm, slot_hbm, x_hbm, cache_hbm, w_hbm, b_hbm, gain_hbm, sw_hbm, rank_hbm)
    targets = (span_ref, res_ref, slot_ref, x_ref, cache_ref, w_ref, b_ref, gain_ref, sw_ref, rank_ref)
    copies = [
        pltpu.make_async_copy(source, target, sems.at[i])
        for i, (source, target) in enumerate(zip(sources, targets))
    ]
    for copy in copies:
        copy.start()
    for copy in copies[:7]:
        copy.wait()
    starts = span_starts(span_ref)
    x = x_ref[...]
    r = iota((ROWS, 128), 0)
    j = iota((ROWS, 128), 1)
    start = jnp.where(r < DEC, r, DEC)
    slot = jnp.full((ROWS, 128), slot_ref[0, DEC], I32)
    res = jnp.full((ROWS, 128), res_ref[0, 0], I32)
    for c in range(1, 4):
        inside = r >= starts[c]
        start = jnp.where(inside, starts[c], start)
        slot = jnp.where(inside, slot_ref[0, DEC + c], slot)
        res = jnp.where(inside, res_ref[0, c], res)
    for d in range(DEC):
        slot = jnp.where(r == d, slot_ref[0, d], slot)
    res = jnp.where(r < DEC, 1, res)
    pos = r - start

    def select(column, line, width):
        return (j == jnp.where(line, column, -1)).astype(F32)[:, 0:width].astype(BF)

    total = b_ref[...] + w_ref[TAPS - 1 : TAPS] * x.astype(F32)
    for lag in range(1, TAPS):
        value = dot(select(r - lag, pos >= lag, ROWS), x)
        for i in range(TAPS - 1):
            old = (pos == i + lag - 3) & (pos < lag) & (res > 0)
            value = value + dot(select(slot, old, SEQ), cache_ref[i])
        total = total + w_ref[TAPS - 1 - lag : TAPS - lag] * value
    cx = silu(total).astype(BF)
    cx_ref[...] = cx
    for copy in copies[7:]:
        copy.wait()
    proj_ref[0:ROWS, 0:512] = dot(cx, rank_ref[...]).astype(BF)
    proj_ref[0:ROWS, 512:640] = jnp.zeros((ROWS, 128), BF)
    proj_ref[0:ROWS, 512 : 512 + 2 * NS] = lax.dot_general(
        cx, sw_ref[...], (((1,), (1,)), ((), ())), preferred_element_type=F32
    ).astype(BF)
    line = 2 * (2 * lax.axis_index("x") + lax.axis_index("core"))
    inverse = 1.0 / (gain_ref[...] * gain_ref[...])
    high = inverse.astype(BF).astype(F32)
    row = iota((16, 512), 0)
    extra = jnp.where(row == line, high, jnp.where(row == line + 1, inverse - high, 0.0))
    proj_ref[ROWS : ROWS + 16, 0:512] = extra.astype(BF)
    proj_ref[ROWS : ROWS + 16, 512:640] = jnp.zeros((16, 128), BF)


def tail_kernel(span_ref, res_ref, slot_ref, x_ref, cache_ref, nc_ref):
    starts = span_starts(span_ref)
    x = x_ref[...]
    group = iota((SEQ, 128), 0)
    j = iota((SEQ, 128), 1)
    length = jnp.ones((SEQ, 128), I32)
    first = jnp.zeros((SEQ, 128), I32)
    kept = jnp.ones((SEQ, 128), I32)
    for s in range(SEQ):
        here = group == slot_ref[0, s]
        if s < DEC:
            first = jnp.where(here, s, first)
        else:
            first = jnp.where(here, starts[s - DEC], first)
            length = jnp.where(here, span_ref[0, s - DEC], length)
            kept = jnp.where(here, res_ref[0, s - DEC], kept)

    def select(column, line, width):
        return (j == jnp.where(line, column, -1)).astype(F32)[:, 0:width].astype(BF)

    for offset in range(TAPS - 1):
        back = length - (TAPS - 1) + offset
        value = dot(select(first + back, back >= 0, ROWS), x)
        for i in range(TAPS - 1):
            old = (back == i - 3) & (kept > 0)
            value = value + dot(select(group, old, SEQ), cache_ref[i])
        nc_ref[offset] = value.astype(BF)


def scan_kernel(
    here_ref, span_ref, res_ref, slot_ref,
    q0_ref, q1_ref, q2_ref, q3_ref, cx_ref, z_ref, gain_ref, sw_ref, sb_ref, dl_ref, skip_ref,
    sc_ref, ow_ref,
    ns_ref, own_ref, sib_ref, inv_ref,
    state_ref, w_vmem, step_ref, drive_ref, bb_ref, cb_ref, pc_ref, tr_ref, sem, state_sem,
):
    fetch = pltpu.make_async_copy(ow_ref, w_vmem, sem)
    fetch.start()
    starts = span_starts(span_ref)
    sums = (
        q0_ref[...].astype(F32) + q1_ref[...].astype(F32)
        + q2_ref[...].astype(F32) + q3_ref[...].astype(F32)
    )
    proj = sums[0:ROWS]
    for t in range(8):
        inverse = sums[ROWS + 2 * t : ROWS + 2 * t + 1, 0:512] + sums[ROWS + 2 * t + 1 : ROWS + 2 * t + 2, 0:512]
        inv_ref[t // 2, :, 512 * (t % 2) : 512 * (t % 2) + 512] = inverse
    low = proj[:, 0:512]
    mean = jnp.mean(low * low, axis=1, keepdims=True)
    norm = (low * lax.rsqrt(mean + EPS) * gain_ref[...]).astype(BF)
    pre = dot(norm, sw_ref[...]) + sb_ref[...]
    step = jnp.maximum(pre, 0.0) + jnp.log1p(jnp.exp(-jnp.abs(pre)))
    values = cx_ref[...].astype(F32)
    step_ref[...] = step
    drive_ref[...] = step * values
    tr_ref[0:ROWS] = proj[:, 512:640]
    tr_ref[ROWS : 2 * ROWS] = jnp.zeros((ROWS, 128), F32)
    turned = tr_ref[...].T
    for r in range(ROWS):
        bb_ref[r] = jnp.broadcast_to(turned[0:NS, r : r + 1], (NS, 128))
        cb_ref[r] = jnp.broadcast_to(turned[NS : 2 * NS, r : r + 1], (NS, 128))
    rate = -jnp.exp(dl_ref[...])
    groups = rate.shape[1] // 128

    def advance(r, state):
        c1 = (r >= starts[1]).astype(I32)
        c2 = (r >= starts[2]).astype(I32)
        c3 = (r >= starts[3]).astype(I32)
        piece = c1 + c2 + c3
        decode = r < DEC
        slot = slot_ref[0, jnp.where(decode, r, DEC + piece)]
        resumed = jnp.where(decode, 1, res_ref[0, piece])
        begins = (r <= DEC) | (r == starts[1]) | (r == starts[2]) | (r == starts[3])
        keep = jnp.where(begins, 0.0, 1.0).astype(F32)
        load = jnp.where(begins, resumed, 0).astype(F32)
        prior = state * keep + sc_ref[slot] * load
        decay = jnp.exp(step_ref[pl.ds(r, 1), :] * rate)
        b = jnp.concatenate([bb_ref[r]] * groups, axis=1)
        c = jnp.concatenate([cb_ref[r]] * groups, axis=1)
        fresh = decay * prior + drive_ref[pl.ds(r, 1), :] * b
        weighed = fresh * c
        pc_ref[r] = weighed[0:8] + weighed[8:16]
        state_ref[slot] = fresh
        return fresh

    lax.fori_loop(0, ROWS, advance, jnp.zeros(rate.shape, F32), unroll=4)
    keep = pltpu.make_async_copy(state_ref, ns_ref, state_sem)
    keep.start()
    output = skip_ref[...] * values
    for k in range(8):
        output = output + pc_ref[:, k, :]
    gated = (output * silu(z_ref[...].astype(F32))).astype(BF)
    fetch.wait()
    x, c = here_ref[0], here_ref[1]
    for out, core in ((own_ref, c), (sib_ref, 1 - c)):
        for k in range(4):
            cols = pl.ds(pl.multiple_of((2 * lax.rem(x + k, 4) + core) * 512, 512), 512)
            out[k] = dot(gated, w_vmem[:, cols]).astype(BF)
    keep.wait()


def pick_kernel(
    here_ref, q0_ref, q1_ref, q2_ref, q3_ref, resid_ref, gain_ref, router_ref, chosen_ref,
    hid_ref, mine_ref, theirs_ref, named_ref,
):
    mixer = (
        q0_ref[...].astype(F32) + q1_ref[...].astype(F32)
        + q2_ref[...].astype(F32) + q3_ref[...].astype(F32)
    ).astype(BF)
    hidden = resid_ref[...].astype(F32) + mixer.astype(F32)
    hid_ref[...] = hidden
    scaled = (hidden * gain_ref[...]).astype(BF)
    wide = scaled.astype(F32)
    lane = iota((ROWS, 128), 1)
    squares = jnp.sum(hidden * hidden, axis=1, keepdims=True)
    stat = jnp.where(lane % 64 == EXPERTS, squares, 0.0)
    for e in range(EXPERTS):
        part = jnp.sum(wide * router_ref[e : e + 1].astype(F32), axis=1, keepdims=True)
        stat = jnp.where(lane % 64 == e, part, stat)
    high = stat.astype(BF).astype(F32)
    stat = jnp.where(lane < 64, high, stat - high).astype(BF)
    for out in (mine_ref, theirs_ref):
        out[0, :, 512:640] = stat[0:CAP]
        out[1, :, 512:640] = jnp.concatenate([stat[CAP:ROWS], jnp.zeros((2 * CAP - ROWS, 128), BF)], axis=0)
    before = (iota((ROWS, ROWS), 0) < iota((ROWS, ROWS), 1)).astype(F32).astype(BF)
    row = iota((CAP, ROWS), 0)
    z, core = here_ref[2], here_ref[1]
    expert = lax.rem(z + 2 * core + iota((8, ROWS), 0), EXPERTS)
    marks = ((chosen_ref[0:1] == expert) | (chosen_ref[1:2] == expert)).astype(F32)
    place = dot(marks.astype(BF), before)
    place = jnp.where(marks > 0.0, place, -1.0).astype(I32)
    for i in range(4):
        hot = (row == place[i : i + 1]).astype(F32).astype(BF)
        out = mine_ref if i < 2 else theirs_ref
        out[i % 2, :, 0:512] = dot(hot, scaled).astype(BF)
    same = (iota((ROWS, ROWS), 0) == iota((ROWS, ROWS), 1)).astype(F32).astype(BF)
    pair = iota((8, ROWS), 0)
    both = jnp.where(pair == 0, chosen_ref[0:1], jnp.where(pair == 1, chosen_ref[1:2], 0))
    turned = lax.dot_general(
        same, both.astype(F32).astype(BF), (((1,), (1,)), ((), ())), preferred_element_type=F32
    )
    named_ref[...] = jnp.zeros_like(named_ref)
    named_ref[:, 0:8] = turned.astype(I32)


def experts_in(here_ref, side, x_ref, inv_ref, wg_ref, wu_ref):
    x = here_ref[0]
    by_row, by_col = jnp.where(side == 0, 4, 1), jnp.where(side == 0, 1, 4)
    both = square = None
    for k in range(4):
        there = lax.rem(x + 4 - k, 4)
        rows = pl.ds(pl.multiple_of(there * 1024, 1024), 1024)
        block = jnp.concatenate([x_ref[j * by_row + k * by_col] for j in range(4)], axis=0)
        part = dot(block, jnp.concatenate([wg_ref[rows, :], wu_ref[rows, :]], axis=1))
        wide = block.astype(F32)
        wide = wide * wide * inv_ref[there]
        square_part = wide[:, 0:128]
        for lane in range(128, 1024, 128):
            square_part = square_part + wide[:, lane : lane + 128]
        if k == 0:
            both, square = part, square_part
        else:
            both, square = both + part, square + square_part
    both = both * lax.rsqrt(jnp.sum(square, axis=1, keepdims=True) / 4096.0 + EPS)
    return (silu(both[:, 0:384]) * both[:, 384:768]).astype(BF)


def experts_out(here_ref, side, act_ref, wd_ref, outs):
    x = here_ref[0]

    def product(rows, there):
        cols = pl.ds(pl.multiple_of(there * 1024, 1024), 1024)
        return dot(rows, wd_ref[:, cols]).astype(BF)

    @pl.when(side == 0)
    def _():
        owners = [j for j in range(4) if (4 - j) % 4 in outs]
        rows = jnp.concatenate([act_ref[96 * j : 96 * j + 96, :] for j in owners], axis=0)
        for n in range(4):
            value = product(rows, lax.rem(x + n, 4))
            for i, j in enumerate(owners):
                outs[(4 - j) % 4][n] = value[96 * i : 96 * i + 96]

    @pl.when(side == 1)
    def _():
        for m in outs:
            value = product(act_ref[...], lax.rem(x + m, 4))
            for j in range(4):
                outs[m][(4 - j) % 4] = value[96 * j : 96 * j + 96]


def ffn_own(here_ref, x_ref, inv_ref, wg_ref, wu_ref, wd_ref, p0_ref, p1_ref, p2_ref, p3_ref, act_ref):
    side = here_ref[1]
    act_ref[...] = experts_in(here_ref, side, x_ref, inv_ref, wg_ref, wu_ref)
    experts_out(here_ref, side, act_ref, wd_ref, {0: p0_ref, 1: p1_ref, 2: p2_ref, 3: p3_ref})


def ffn_other(here_ref, x_ref, inv_ref, wg_ref, wu_ref, wd_ref, earlier_ref, act_ref, p2_ref):
    side = 1 - here_ref[1]
    act_ref[...] = experts_in(here_ref, side, x_ref, inv_ref, wg_ref, wu_ref)
    experts_out(here_ref, side, act_ref, wd_ref, {2: p2_ref})


def ffn_rest(here_ref, act_ref, wd_ref, p0_ref, p1_ref, p3_ref):
    experts_out(here_ref, 1 - here_ref[1], act_ref, wd_ref, {1: p1_ref, 3: p3_ref, 0: p0_ref})


def final_kernel(
    here_ref, mine_ref, theirs_ref, stat_ref, hid_ref, chosen_ref, out_ref,
):
    stat = stat_ref[0:ROWS].astype(F32)

    def column(e):
        return stat[:, e : e + 1] + stat[:, 64 + e : 65 + e]

    scale = lax.rsqrt(column(EXPERTS) / 4096.0 + EPS)
    e0, e1 = chosen_ref[:, 0:1], chosen_ref[:, 1:2]
    l0 = jnp.zeros((ROWS, 1), F32)
    l1 = jnp.zeros((ROWS, 1), F32)
    for e in range(EXPERTS):
        l0 = l0 + jnp.where(e0 == e, column(e), 0.0)
        l1 = l1 + jnp.where(e1 == e, column(e), 0.0)
    gap = (l0 - l1) * scale
    route0 = 1.0 / (1.0 + jnp.exp(-gap))
    route1 = 1.0 / (1.0 + jnp.exp(gap))
    before = (iota((ROWS, ROWS), 1) < iota((ROWS, ROWS), 0)).astype(F32).astype(BF)
    lane = iota((ROWS, CAP), 1)
    total = hid_ref[...]
    z, core = here_ref[2], here_ref[1]
    expert = lax.rem(z + 2 * core + iota((ROWS, 128), 1), EXPERTS)
    first, second = e0 == expert, e1 == expert
    marks = (first | second).astype(F32)
    place = dot(before, marks.astype(BF))
    place = jnp.where(marks > 0.0, place, -1.0).astype(I32)
    weight = jnp.where(first, route0, jnp.where(second, route1, 0.0))
    for i in range(4):
        hot = (lane == place[:, i : i + 1]).astype(F32).astype(BF)
        ref = mine_ref if i < 2 else theirs_ref
        total = total + weight[:, i : i + 1] * dot(hot, ref[i % 2])
    out_ref[...] = total.astype(BF)


def move(value, axis, shift):
    size = lax.axis_size(axis)
    return lax.ppermute(value, axis, [(i, (i + shift) % size) for i in range(size)])


def by_core(value, first, second):
    sizes = tuple(lax.axis_size(name) for name in AXES)
    pairs = []
    for source in range(int(np.prod(sizes))):
        place = list(np.unravel_index(source, sizes))
        axis, shift = (first, second)[int(place[3])]
        at = AXES.index(axis)
        place[at] = (place[at] + shift) % sizes[at]
        pairs.append((source, int(np.ravel_multi_index(place, sizes))))
    return lax.ppermute(value, AXES, pairs)


def across(value, shift):
    return by_core(value, ("x", shift), ("y", shift))


def along(value, shift):
    return by_core(value, ("y", shift), ("x", shift))


def summed(*values):
    total = values[0].astype(F32)
    for value in values[1:]:
        total = total + value.astype(F32)
    return total[..., 0:64] + total[..., 64:128]


def coded(value):
    high = value.astype(BF)
    low = (value - high.astype(F32)).astype(BF)
    return jnp.concatenate([high, low], axis=-1)


def add(*values):
    total = values[0].astype(F32)
    for value in values[1:]:
        total = total + value.astype(F32)
    return total.astype(BF)


def stay(value):
    return pltpu.with_memory_space_constraint(value, pltpu.HBM)


def call(kernel, outs, ins, mib, scratch=(), flops=0, moved=0, name=None, out_specs=None):
    single = not isinstance(outs, (list, tuple))
    return pl.pallas_call(
        kernel,
        out_shape=outs,
        in_specs=ins,
        out_specs=out_specs or (VMEM if single else [VMEM] * len(outs)),
        scratch_shapes=list(scratch),
        compiler_params=params(mib),
        cost_estimate=pl.CostEstimate(flops=flops, bytes_accessed=moved, transcendentals=0),
        name=name,
    )


def shape(dims, dtype):
    return jax.ShapeDtypeStruct(dims, dtype)


def per_device(
    conv_input, gate_input, conv_cache, state_cache, span_lengths, span_resumes, slot_index,
    conv_weight, conv_bias, rank_weight, state_weight, step_gain, step_weight, step_bias,
    decay_log, skip_gain, out_weight, residual, moe_gain, router_weight, chosen_experts,
    gate_weight, up_weight, down_weight,
):
    here = jnp.stack(
        [lax.axis_index("x"), lax.axis_index("core"), lax.axis_index("z")]
    ).astype(I32)
    even = lax.axis_index("core") == 0
    old = conv_cache.transpose(1, 0, 2)
    cx, proj = call(
        conv_kernel,
        [shape((ROWS, 1024), BF), shape((ROWS + 16, 640), BF)],
        [HBM] * 10,
        16,
        [
            pltpu.SMEM((1, 4), I32),
            pltpu.SMEM((1, 4), I32),
            pltpu.SMEM((1, SEQ), I32),
            pltpu.VMEM((ROWS, 1024), BF),
            pltpu.VMEM((3, SEQ, 1024), BF),
            pltpu.VMEM((TAPS, 1024), F32),
            pltpu.VMEM((1, 1024), F32),
            pltpu.VMEM((1024, 512), BF),
            pltpu.VMEM((2 * NS, 1024), BF),
            pltpu.VMEM((1, 512), F32),
            pltpu.SemaphoreType.DMA((10,)),
        ],
        flops=10**9,
        moved=2 * 10**6,
        name="conv",
    )(
        *map(
            stay,
            (
                span_lengths, span_resumes, slot_index, conv_input,
                old, conv_weight, conv_bias.reshape(1, 1024),
                rank_weight, state_weight.T, moe_gain.reshape(1, 512),
            ),
        )
    )
    new_conv = call(
        tail_kernel,
        shape((3, SEQ, 1024), BF),
        [SMEM] * 3 + [VMEM] * 2,
        8,
        flops=10**9,
        moved=10**6,
        name="tail",
    )(span_lengths, span_resumes, slot_index, conv_input, old)
    chip = add(proj, move(proj, "core", 1))
    parts = [chip] + [move(chip, "x", k) for k in (1, 2, 3)]
    new_state, own, sib, inverse = call(
        scan_kernel,
        [
            shape((SEQ, NS, 1024), F32),
            shape((4, ROWS, 512), BF),
            shape((4, ROWS, 512), BF),
            shape((4, 1, 1024), F32),
        ],
        [SMEM] * 4 + [VMEM] * 12 + [HBM],
        32,
        [
            pltpu.VMEM((SEQ, NS, 1024), F32),
            pltpu.VMEM((1024, 4096), BF),
            pltpu.VMEM((ROWS, 1024), F32),
            pltpu.VMEM((ROWS, 1024), F32),
            pltpu.VMEM((ROWS, NS, 128), F32),
            pltpu.VMEM((ROWS, NS, 128), F32),
            pltpu.VMEM((ROWS, 8, 1024), F32),
            pltpu.VMEM((128, 128), F32),
            pltpu.SemaphoreType.DMA,
            pltpu.SemaphoreType.DMA,
        ],
        flops=10**9,
        moved=10**7,
        name="scan",
        out_specs=[HBM] + [VMEM] * 3,
    )(
        here, span_lengths, span_resumes, slot_index, *parts, cx, gate_input,
        step_gain.reshape(1, 512), step_weight, step_bias.reshape(1, 1024), decay_log,
        skip_gain.reshape(1, 1024), state_cache, stay(out_weight),
    )
    mixed = add(own, move(sib, "core", 1))
    parts = [mixed[0]] + [move(mixed[k], "x", k) for k in (1, 2, 3)]
    hidden, mine, theirs, named = call(
        pick_kernel,
        [
            shape((ROWS, 512), F32),
            shape((2, CAP, 640), BF),
            shape((2, CAP, 640), BF),
            shape((ROWS, 128), I32),
        ],
        [SMEM] + [VMEM] * 8,
        8,
        flops=10**8,
        moved=10**6,
        name="pick",
    )(here, *parts, residual, moe_gain.reshape(1, 512), router_weight.T, chosen_experts.T)
    theirs = move(theirs, "core", 1)
    stat = coded(summed(mine[:, :, 512:640], theirs[:, :, 512:640])).reshape(2 * CAP, 128)
    mine, theirs = mine[:, :, 0:512], theirs[:, :, 0:512]
    rows = jnp.concatenate([jnp.where(even, mine, theirs), jnp.where(even, theirs, mine)], axis=2)
    later = by_core(rows[1], ("z", 1), ("z", 3))
    sooner = by_core(rows[0], ("z", 0), ("z", 2))
    rows = jnp.concatenate([jnp.concatenate([sooner, later], axis=0), stat], axis=1)
    rows1, rows3 = across(rows, 1), across(rows, 3)
    rows2 = jnp.concatenate([across(rows1[0:CAP], 1), across(rows3[CAP : 2 * CAP], 3)], axis=0)
    stat = coded(summed(*[part[:, 1024:1152] for part in (rows, rows1, rows2, rows3)]))
    upper = jnp.stack([rows[:, 0:1024], rows1[:, 0:1024]])
    lower = jnp.stack([rows2[:, 0:1024], rows3[:, 0:1024]])
    upper1, lower3 = along(upper, 1), along(lower, 3)
    lower1, upper3 = along(lower, 1), along(upper, 3)
    upper2, lower2 = along(upper1, 1), along(lower3, 3)
    mine = jnp.concatenate(
        [upper, lower, upper1, lower1, upper2, lower2, upper3, lower3], axis=0
    )
    theirs = move(mine, "core", 1)
    gate, up, down = gate_weight[0], up_weight[0], down_weight[0]
    block = shape((4, 96, 1024), BF)

    mine = call(
        ffn_own,
        [block] * 4,
        [SMEM] + [VMEM] * 5,
        30,
        [pltpu.VMEM((384, 384), BF)],
        flops=6 * 384 * 2048 * 768,
        moved=12 * 10**6,
        name="experts_own",
    )(here, mine, inverse, gate, up, down)
    act, theirs2 = call(
        ffn_other,
        [shape((384, 384), BF), block],
        [SMEM] + [VMEM] * 6,
        28,
        flops=5 * 384 * 2048 * 768,
        moved=10 * 10**6,
        name="experts_other",
    )(here, theirs, inverse, gate, up, down, mine[0])
    theirs = call(
        ffn_rest,
        [block] * 3,
        [SMEM] + [VMEM] * 2,
        20,
        flops=384 * 3072 * 768,
        moved=5 * 10**6,
        name="experts_rest",
    )(here, act, down)
    part2 = add(mine[2], move(theirs2, "core", 1))
    far1, far3 = along(part2[0:2], 1), along(part2[2:4], 3)
    part1 = add(mine[1], move(theirs[1], "core", 1))
    part3 = add(mine[3], move(theirs[2], "core", 1))
    part0 = add(mine[0], move(theirs[0], "core", 1))
    near1, near3 = along(part1[2:4], 1), along(part3[0:2], 3)
    next1, next3 = along(add(part1[0:2], far1), 1), along(add(part3[2:4], far3), 3)
    lines = jnp.concatenate(
        [add(part0[0:2], next1, near3), add(part0[2:4], near1, next3)], axis=0
    )
    lines = add(lines[0], *[across(lines[k], k) for k in (1, 2, 3)])
    later = by_core(lines[CAP : 2 * CAP], ("z", 3), ("z", 1))
    sooner = by_core(lines[0:CAP], ("z", 0), ("z", 2))
    lines = jnp.stack([sooner, later])
    left, right = lines[:, :, 0:512], lines[:, :, 512:1024]
    mine = jnp.where(even, left, right)
    theirs = jnp.concatenate([jnp.where(even, right, left), stat.reshape(2, CAP, 128)], axis=2)
    theirs = move(theirs, "core", 1)
    stat = jnp.where(even, stat, theirs[:, :, 512:640].reshape(2 * CAP, 128))
    theirs = theirs[:, :, 0:512]
    out = call(
        final_kernel,
        shape((ROWS, 512), BF),
        [SMEM] + [VMEM] * 5,
        8,
        flops=10**8,
        moved=10**6,
        name="combine",
    )(here, mine, theirs, stat, hidden, named)
    new_conv = new_conv.transpose(1, 0, 2)
    return (out, new_state, new_conv)


def solution(mesh):
    grid = Mesh(mesh.devices.reshape(4, 4, 4, 2), AXES)
    group, tensor = ("z", "y"), ("x", "core")
    return jax.shard_map(
        per_device,
        mesh=grid,
        in_specs=(
            P(group, tensor),
            P(group, tensor),
            P(group, None, tensor),
            P(group, None, tensor),
            P(group, None),
            P(group, None),
            P(group, None),
            P(None, tensor),
            P(tensor),
            P(tensor, None),
            P(tensor, None),
            P(),
            P(None, tensor),
            P(tensor),
            P(None, tensor),
            P(tensor),
            P(tensor, None),
            P(group, tensor),
            P(tensor),
            P(tensor, None),
            P(group, None),
            P(group, None, tensor),
            P(group, None, tensor),
            P(group, tensor, None),
        ),
        out_specs=(P(group, tensor), P(group, None, tensor), P(group, None, tensor)),
        check_vma=False,
    )
```

```python
import functools

import jax
import jax.numpy as jnp
import numpy as np
from jax import lax
from jax.experimental import pallas as pl
from jax.experimental.pallas import tpu as pltpu
from jax.sharding import Mesh
from jax.sharding import PartitionSpec as P

DEC = 16
ROWS = 64
SEQ = 20
CAP = 48
NS = 16
TAPS = 4
EXPERTS = 4
EPS = 1e-6
BF = jnp.bfloat16
F32 = jnp.float32
I32 = jnp.int32
VMEM = pl.BlockSpec(memory_space=pltpu.VMEM)
SMEM = pl.BlockSpec(memory_space=pltpu.SMEM)
HBM = pl.BlockSpec(memory_space=pltpu.HBM)
AXES = ("z", "y", "x", "core")


def params(mib):
    return pltpu.CompilerParams(vmem_limit_bytes=mib * 1024 * 1024)


def iota(shape, dim):
    return lax.broadcasted_iota(I32, shape, dim)


def silu(v):
    return v / (1.0 + jnp.exp(-v))


def dot(a, b):
    return jnp.dot(a, b, preferred_element_type=F32)


def span_starts(span_ref):
    s1 = DEC + span_ref[0, 0]
    s2 = s1 + span_ref[0, 1]
    s3 = s2 + span_ref[0, 2]
    return (jnp.int32(DEC), s1, s2, s3)


def conv_kernel(
    span_hbm, res_hbm, slot_hbm, x_hbm, cache_hbm, w_hbm, b_hbm, rank_hbm, sw_hbm, gain_hbm,
    cx_ref, proj_ref,
    span_ref, res_ref, slot_ref, x_ref, cache_ref, w_ref, b_ref, rank_ref, sw_ref, gain_ref, sems,
):
    sources = (span_hbm, res_hbm, slot_hbm, x_hbm, cache_hbm, w_hbm, b_hbm, gain_hbm, sw_hbm, rank_hbm)
    targets = (span_ref, res_ref, slot_ref, x_ref, cache_ref, w_ref, b_ref, gain_ref, sw_ref, rank_ref)
    copies = [
        pltpu.make_async_copy(source, target, sems.at[i])
        for i, (source, target) in enumerate(zip(sources, targets))
    ]
    for copy in copies:
        copy.start()
    for copy in copies[:7]:
        copy.wait()
    starts = span_starts(span_ref)
    x = x_ref[...]
    r = iota((ROWS, 128), 0)
    j = iota((ROWS, 128), 1)
    start = jnp.where(r < DEC, r, DEC)
    slot = jnp.full((ROWS, 128), slot_ref[0, DEC], I32)
    res = jnp.full((ROWS, 128), res_ref[0, 0], I32)
    for c in range(1, 4):
        inside = r >= starts[c]
        start = jnp.where(inside, starts[c], start)
        slot = jnp.where(inside, slot_ref[0, DEC + c], slot)
        res = jnp.where(inside, res_ref[0, c], res)
    for d in range(DEC):
        slot = jnp.where(r == d, slot_ref[0, d], slot)
    res = jnp.where(r < DEC, 1, res)
    pos = r - start

    def select(column, line, width):
        return (j == jnp.where(line, column, -1)).astype(F32)[:, 0:width].astype(BF)

    total = b_ref[...] + w_ref[TAPS - 1 : TAPS] * x.astype(F32)
    for lag in range(1, TAPS):
        value = dot(select(r - lag, pos >= lag, ROWS), x)
        for i in range(TAPS - 1):
            old = (pos == i + lag - 3) & (pos < lag) & (res > 0)
            value = value + dot(select(slot, old, SEQ), cache_ref[i])
        total = total + w_ref[TAPS - 1 - lag : TAPS - lag] * value
    cx = silu(total).astype(BF)
    cx_ref[...] = cx
    for copy in copies[7:]:
        copy.wait()
    proj_ref[0:ROWS, 0:512] = dot(cx, rank_ref[...]).astype(BF)
    proj_ref[0:ROWS, 512:640] = jnp.zeros((ROWS, 128), BF)
    proj_ref[0:ROWS, 512 : 512 + 2 * NS] = lax.dot_general(
        cx, sw_ref[...], (((1,), (1,)), ((), ())), preferred_element_type=F32
    ).astype(BF)
    line = 2 * (2 * lax.axis_index("x") + lax.axis_index("core"))
    inverse = 1.0 / (gain_ref[...] * gain_ref[...])
    high = inverse.astype(BF).astype(F32)
    row = iota((16, 512), 0)
    extra = jnp.where(row == line, high, jnp.where(row == line + 1, inverse - high, 0.0))
    proj_ref[ROWS : ROWS + 16, 0:512] = extra.astype(BF)
    proj_ref[ROWS : ROWS + 16, 512:640] = jnp.zeros((16, 128), BF)


def tail_kernel(span_ref, res_ref, slot_ref, x_ref, cache_ref, nc_ref):
    starts = span_starts(span_ref)
    x = x_ref[...]
    group = iota((SEQ, 128), 0)
    j = iota((SEQ, 128), 1)
    length = jnp.ones((SEQ, 128), I32)
    first = jnp.zeros((SEQ, 128), I32)
    kept = jnp.ones((SEQ, 128), I32)
    for s in range(SEQ):
        here = group == slot_ref[0, s]
        if s < DEC:
            first = jnp.where(here, s, first)
        else:
            first = jnp.where(here, starts[s - DEC], first)
            length = jnp.where(here, span_ref[0, s - DEC], length)
            kept = jnp.where(here, res_ref[0, s - DEC], kept)

    def select(column, line, width):
        return (j == jnp.where(line, column, -1)).astype(F32)[:, 0:width].astype(BF)

    for offset in range(TAPS - 1):
        back = length - (TAPS - 1) + offset
        value = dot(select(first + back, back >= 0, ROWS), x)
        for i in range(TAPS - 1):
            old = (back == i - 3) & (kept > 0)
            value = value + dot(select(group, old, SEQ), cache_ref[i])
        nc_ref[offset] = value.astype(BF)


def scan_kernel(
    here_ref, span_ref, res_ref, slot_ref,
    q0_ref, q1_ref, q2_ref, q3_ref, cx_ref, z_ref, gain_ref, sw_ref, sb_ref, dl_ref, skip_ref,
    sc_ref, ow_ref,
    ns_ref, own_ref, sib_ref, inv_ref,
    state_ref, w_vmem, step_ref, drive_ref, bb_ref, cb_ref, pc_ref, tr_ref, sem, state_sem,
):
    fetch = pltpu.make_async_copy(ow_ref, w_vmem, sem)
    fetch.start()
    starts = span_starts(span_ref)
    sums = (
        q0_ref[...].astype(F32) + q1_ref[...].astype(F32)
        + q2_ref[...].astype(F32) + q3_ref[...].astype(F32)
    )
    proj = sums[0:ROWS]
    for t in range(8):
        inverse = sums[ROWS + 2 * t : ROWS + 2 * t + 1, 0:512] + sums[ROWS + 2 * t + 1 : ROWS + 2 * t + 2, 0:512]
        inv_ref[t // 2, :, 512 * (t % 2) : 512 * (t % 2) + 512] = inverse
    low = proj[:, 0:512]
    mean = jnp.mean(low * low, axis=1, keepdims=True)
    norm = (low * lax.rsqrt(mean + EPS) * gain_ref[...]).astype(BF)
    pre = dot(norm, sw_ref[...]) + sb_ref[...]
    step = jnp.maximum(pre, 0.0) + jnp.log1p(jnp.exp(-jnp.abs(pre)))
    values = cx_ref[...].astype(F32)
    step_ref[...] = step
    drive_ref[...] = step * values
    tr_ref[0:ROWS] = proj[:, 512:640]
    tr_ref[ROWS : 2 * ROWS] = jnp.zeros((ROWS, 128), F32)
    turned = tr_ref[...].T
    for r in range(ROWS):
        bb_ref[r] = jnp.broadcast_to(turned[0:NS, r : r + 1], (NS, 128))
        cb_ref[r] = jnp.broadcast_to(turned[NS : 2 * NS, r : r + 1], (NS, 128))
    rate = -jnp.exp(dl_ref[...])
    groups = rate.shape[1] // 128

    def advance(r, state):
        c1 = (r >= starts[1]).astype(I32)
        c2 = (r >= starts[2]).astype(I32)
        c3 = (r >= starts[3]).astype(I32)
        piece = c1 + c2 + c3
        decode = r < DEC
        slot = slot_ref[0, jnp.where(decode, r, DEC + piece)]
        resumed = jnp.where(decode, 1, res_ref[0, piece])
        begins = (r <= DEC) | (r == starts[1]) | (r == starts[2]) | (r == starts[3])
        keep = jnp.where(begins, 0.0, 1.0).astype(F32)
        load = jnp.where(begins, resumed, 0).astype(F32)
        prior = state * keep + sc_ref[slot] * load
        decay = jnp.exp(step_ref[pl.ds(r, 1), :] * rate)
        b = jnp.concatenate([bb_ref[r]] * groups, axis=1)
        c = jnp.concatenate([cb_ref[r]] * groups, axis=1)
        fresh = decay * prior + drive_ref[pl.ds(r, 1), :] * b
        weighed = fresh * c
        pc_ref[r] = weighed[0:8] + weighed[8:16]
        state_ref[slot] = fresh
        return fresh

    lax.fori_loop(0, ROWS, advance, jnp.zeros(rate.shape, F32), unroll=4)
    keep = pltpu.make_async_copy(state_ref, ns_ref, state_sem)
    keep.start()
    output = skip_ref[...] * values
    for k in range(8):
        output = output + pc_ref[:, k, :]
    gated = (output * silu(z_ref[...].astype(F32))).astype(BF)
    fetch.wait()
    x, c = here_ref[0], here_ref[1]
    for out, core in ((own_ref, c), (sib_ref, 1 - c)):
        for k in range(4):
            cols = pl.ds(pl.multiple_of((2 * lax.rem(x + k, 4) + core) * 512, 512), 512)
            out[k] = dot(gated, w_vmem[:, cols]).astype(BF)
    keep.wait()


def pick_kernel(
    here_ref, q0_ref, q1_ref, q2_ref, q3_ref, resid_ref, gain_ref, router_ref, chosen_ref,
    hid_ref, mine_ref, theirs_ref, named_ref,
):
    mixer = (
        q0_ref[...].astype(F32) + q1_ref[...].astype(F32)
        + q2_ref[...].astype(F32) + q3_ref[...].astype(F32)
    ).astype(BF)
    hidden = resid_ref[...].astype(F32) + mixer.astype(F32)
    hid_ref[...] = hidden
    scaled = (hidden * gain_ref[...]).astype(BF)
    wide = scaled.astype(F32)
    lane = iota((ROWS, 128), 1)
    squares = jnp.sum(hidden * hidden, axis=1, keepdims=True)
    stat = jnp.where(lane % 64 == EXPERTS, squares, 0.0)
    for e in range(EXPERTS):
        part = jnp.sum(wide * router_ref[e : e + 1].astype(F32), axis=1, keepdims=True)
        stat = jnp.where(lane % 64 == e, part, stat)
    high = stat.astype(BF).astype(F32)
    stat = jnp.where(lane < 64, high, stat - high).astype(BF)
    for out in (mine_ref, theirs_ref):
        out[0, :, 512:640] = stat[0:CAP]
        out[1, :, 512:640] = jnp.concatenate([stat[CAP:ROWS], jnp.zeros((2 * CAP - ROWS, 128), BF)], axis=0)
    before = (iota((ROWS, ROWS), 0) < iota((ROWS, ROWS), 1)).astype(F32).astype(BF)
    row = iota((CAP, ROWS), 0)
    z, core = here_ref[2], here_ref[1]
    expert = lax.rem(z + 2 * core + iota((8, ROWS), 0), EXPERTS)
    marks = ((chosen_ref[0:1] == expert) | (chosen_ref[1:2] == expert)).astype(F32)
    place = dot(marks.astype(BF), before)
    place = jnp.where(marks > 0.0, place, -1.0).astype(I32)
    for i in range(4):
        hot = (row == place[i : i + 1]).astype(F32).astype(BF)
        out = mine_ref if i < 2 else theirs_ref
        out[i % 2, :, 0:512] = dot(hot, scaled).astype(BF)
    same = (iota((ROWS, ROWS), 0) == iota((ROWS, ROWS), 1)).astype(F32).astype(BF)
    pair = iota((8, ROWS), 0)
    both = jnp.where(pair == 0, chosen_ref[0:1], jnp.where(pair == 1, chosen_ref[1:2], 0))
    turned = lax.dot_general(
        same, both.astype(F32).astype(BF), (((1,), (1,)), ((), ())), preferred_element_type=F32
    )
    named_ref[...] = jnp.zeros_like(named_ref)
    named_ref[:, 0:8] = turned.astype(I32)


def experts_in(here_ref, side, x_ref, inv_ref, wg_ref, wu_ref):
    x = here_ref[0]
    by_row, by_col = jnp.where(side == 0, 4, 1), jnp.where(side == 0, 1, 4)
    both = square = None
    for k in range(4):
        there = lax.rem(x + 4 - k, 4)
        rows = pl.ds(pl.multiple_of(there * 1024, 1024), 1024)
        block = jnp.concatenate([x_ref[j * by_row + k * by_col] for j in range(4)], axis=0)
        part = dot(block, jnp.concatenate([wg_ref[rows, :], wu_ref[rows, :]], axis=1))
        wide = block.astype(F32)
        wide = wide * wide * inv_ref[there]
        square_part = wide[:, 0:128]
        for lane in range(128, 1024, 128):
            square_part = square_part + wide[:, lane : lane + 128]
        if k == 0:
            both, square = part, square_part
        else:
            both, square = both + part, square + square_part
    both = both * lax.rsqrt(jnp.sum(square, axis=1, keepdims=True) / 4096.0 + EPS)
    return (silu(both[:, 0:384]) * both[:, 384:768]).astype(BF)


def experts_out(here_ref, side, act_ref, wd_ref, outs):
    x = here_ref[0]

    def product(rows, there):
        cols = pl.ds(pl.multiple_of(there * 1024, 1024), 1024)
        return dot(rows, wd_ref[:, cols]).astype(BF)

    @pl.when(side == 0)
    def _():
        owners = [j for j in range(4) if (4 - j) % 4 in outs]
        rows = jnp.concatenate([act_ref[96 * j : 96 * j + 96, :] for j in owners], axis=0)
        for n in range(4):
            value = product(rows, lax.rem(x + n, 4))
            for i, j in enumerate(owners):
                outs[(4 - j) % 4][n] = value[96 * i : 96 * i + 96]

    @pl.when(side == 1)
    def _():
        for m in outs:
            value = product(act_ref[...], lax.rem(x + m, 4))
            for j in range(4):
                outs[m][(4 - j) % 4] = value[96 * j : 96 * j + 96]


def ffn_own(here_ref, x_ref, inv_ref, wg_ref, wu_ref, wd_ref, p0_ref, p1_ref, p2_ref, p3_ref, act_ref):
    side = here_ref[1]
    act_ref[...] = experts_in(here_ref, side, x_ref, inv_ref, wg_ref, wu_ref)
    experts_out(here_ref, side, act_ref, wd_ref, {0: p0_ref, 1: p1_ref, 2: p2_ref, 3: p3_ref})


def ffn_other(here_ref, x_ref, inv_ref, wg_ref, wu_ref, wd_ref, earlier_ref, act_ref, p2_ref):
    side = 1 - here_ref[1]
    act_ref[...] = experts_in(here_ref, side, x_ref, inv_ref, wg_ref, wu_ref)
    experts_out(here_ref, side, act_ref, wd_ref, {2: p2_ref})


def ffn_rest(here_ref, act_ref, wd_ref, p0_ref, p1_ref, p3_ref):
    experts_out(here_ref, 1 - here_ref[1], act_ref, wd_ref, {1: p1_ref, 3: p3_ref, 0: p0_ref})


def final_kernel(
    here_ref, mine_ref, theirs_ref, stat_ref, hid_ref, chosen_ref, out_ref,
):
    stat = stat_ref[0:ROWS].astype(F32)

    def column(e):
        return stat[:, e : e + 1] + stat[:, 64 + e : 65 + e]

    scale = lax.rsqrt(column(EXPERTS) / 4096.0 + EPS)
    e0, e1 = chosen_ref[:, 0:1], chosen_ref[:, 1:2]
    l0 = jnp.zeros((ROWS, 1), F32)
    l1 = jnp.zeros((ROWS, 1), F32)
    for e in range(EXPERTS):
        l0 = l0 + jnp.where(e0 == e, column(e), 0.0)
        l1 = l1 + jnp.where(e1 == e, column(e), 0.0)
    gap = (l0 - l1) * scale
    route0 = 1.0 / (1.0 + jnp.exp(-gap))
    route1 = 1.0 / (1.0 + jnp.exp(gap))
    before = (iota((ROWS, ROWS), 1) < iota((ROWS, ROWS), 0)).astype(F32).astype(BF)
    lane = iota((ROWS, CAP), 1)
    total = hid_ref[...]
    z, core = here_ref[2], here_ref[1]
    expert = lax.rem(z + 2 * core + iota((ROWS, 128), 1), EXPERTS)
    first, second = e0 == expert, e1 == expert
    marks = (first | second).astype(F32)
    place = dot(before, marks.astype(BF))
    place = jnp.where(marks > 0.0, place, -1.0).astype(I32)
    weight = jnp.where(first, route0, jnp.where(second, route1, 0.0))
    for i in range(4):
        hot = (lane == place[:, i : i + 1]).astype(F32).astype(BF)
        ref = mine_ref if i < 2 else theirs_ref
        total = total + weight[:, i : i + 1] * dot(hot, ref[i % 2])
    out_ref[...] = total.astype(BF)


def move(value, axis, shift):
    size = lax.axis_size(axis)
    return lax.ppermute(value, axis, [(i, (i + shift) % size) for i in range(size)])


def by_core(value, first, second):
    sizes = tuple(lax.axis_size(name) for name in AXES)
    pairs = []
    for source in range(int(np.prod(sizes))):
        place = list(np.unravel_index(source, sizes))
        axis, shift = (first, second)[int(place[3])]
        at = AXES.index(axis)
        place[at] = (place[at] + shift) % sizes[at]
        pairs.append((source, int(np.ravel_multi_index(place, sizes))))
    return lax.ppermute(value, AXES, pairs)


def across(value, shift):
    return by_core(value, ("x", shift), ("y", shift))


def along(value, shift):
    return by_core(value, ("y", shift), ("x", shift))


def summed(*values):
    total = values[0].astype(F32)
    for value in values[1:]:
        total = total + value.astype(F32)
    return total[..., 0:64] + total[..., 64:128]


def coded(value):
    high = value.astype(BF)
    low = (value - high.astype(F32)).astype(BF)
    return jnp.concatenate([high, low], axis=-1)


def add(*values):
    total = values[0].astype(F32)
    for value in values[1:]:
        total = total + value.astype(F32)
    return total.astype(BF)


def stay(value):
    return pltpu.with_memory_space_constraint(value, pltpu.HBM)


def call(kernel, outs, ins, mib, scratch=(), flops=0, moved=0, name=None, out_specs=None):
    single = not isinstance(outs, (list, tuple))
    return pl.pallas_call(
        kernel,
        out_shape=outs,
        in_specs=ins,
        out_specs=out_specs or (VMEM if single else [VMEM] * len(outs)),
        scratch_shapes=list(scratch),
        compiler_params=params(mib),
        cost_estimate=pl.CostEstimate(flops=flops, bytes_accessed=moved, transcendentals=0),
        name=name,
    )


def shape(dims, dtype):
    return jax.ShapeDtypeStruct(dims, dtype)


def per_device(
    conv_input, gate_input, conv_cache, state_cache, span_lengths, span_resumes, slot_index,
    conv_weight, conv_bias, rank_weight, state_weight, step_gain, step_weight, step_bias,
    decay_log, skip_gain, out_weight, residual, moe_gain, router_weight, chosen_experts,
    gate_weight, up_weight, down_weight,
):
    here = jnp.stack(
        [lax.axis_index("x"), lax.axis_index("core"), lax.axis_index("z")]
    ).astype(I32)
    even = lax.axis_index("core") == 0
    old = conv_cache.transpose(1, 0, 2)
    cx, proj = call(
        conv_kernel,
        [shape((ROWS, 1024), BF), shape((ROWS + 16, 640), BF)],
        [HBM] * 10,
        16,
        [
            pltpu.SMEM((1, 4), I32),
            pltpu.SMEM((1, 4), I32),
            pltpu.SMEM((1, SEQ), I32),
            pltpu.VMEM((ROWS, 1024), BF),
            pltpu.VMEM((3, SEQ, 1024), BF),
            pltpu.VMEM((TAPS, 1024), F32),
            pltpu.VMEM((1, 1024), F32),
            pltpu.VMEM((1024, 512), BF),
            pltpu.VMEM((2 * NS, 1024), BF),
            pltpu.VMEM((1, 512), F32),
            pltpu.SemaphoreType.DMA((10,)),
        ],
        flops=10**9,
        moved=2 * 10**6,
        name="conv",
    )(
        *map(
            stay,
            (
                span_lengths, span_resumes, slot_index, conv_input,
                old, conv_weight, conv_bias.reshape(1, 1024),
                rank_weight, state_weight.T, moe_gain.reshape(1, 512),
            ),
        )
    )
    new_conv = call(
        tail_kernel,
        shape((3, SEQ, 1024), BF),
        [SMEM] * 3 + [VMEM] * 2,
        8,
        flops=10**9,
        moved=10**6,
        name="tail",
    )(span_lengths, span_resumes, slot_index, conv_input, old)
    chip = add(proj, move(proj, "core", 1))
    parts = [chip] + [move(chip, "x", k) for k in (1, 2, 3)]
    new_state, own, sib, inverse = call(
        scan_kernel,
        [
            shape((SEQ, NS, 1024), F32),
            shape((4, ROWS, 512), BF),
            shape((4, ROWS, 512), BF),
            shape((4, 1, 1024), F32),
        ],
        [SMEM] * 4 + [VMEM] * 12 + [HBM],
        32,
        [
            pltpu.VMEM((SEQ, NS, 1024), F32),
            pltpu.VMEM((1024, 4096), BF),
            pltpu.VMEM((ROWS, 1024), F32),
            pltpu.VMEM((ROWS, 1024), F32),
            pltpu.VMEM((ROWS, NS, 128), F32),
            pltpu.VMEM((ROWS, NS, 128), F32),
            pltpu.VMEM((ROWS, 8, 1024), F32),
            pltpu.VMEM((128, 128), F32),
            pltpu.SemaphoreType.DMA,
            pltpu.SemaphoreType.DMA,
        ],
        flops=10**9,
        moved=10**7,
        name="scan",
        out_specs=[HBM] + [VMEM] * 3,
    )(
        here, span_lengths, span_resumes, slot_index, *parts, cx, gate_input,
        step_gain.reshape(1, 512), step_weight, step_bias.reshape(1, 1024), decay_log,
        skip_gain.reshape(1, 1024), state_cache, stay(out_weight),
    )
    mixed = add(own, move(sib, "core", 1))
    parts = [mixed[0]] + [move(mixed[k], "x", k) for k in (1, 2, 3)]
    hidden, mine, theirs, named = call(
        pick_kernel,
        [
            shape((ROWS, 512), F32),
            shape((2, CAP, 640), BF),
            shape((2, CAP, 640), BF),
            shape((ROWS, 128), I32),
        ],
        [SMEM] + [VMEM] * 8,
        8,
        flops=10**8,
        moved=10**6,
        name="pick",
    )(here, *parts, residual, moe_gain.reshape(1, 512), router_weight.T, chosen_experts.T)
    theirs = move(theirs, "core", 1)
    stat = coded(summed(mine[:, :, 512:640], theirs[:, :, 512:640])).reshape(2 * CAP, 128)
    mine, theirs = mine[:, :, 0:512], theirs[:, :, 0:512]
    rows = jnp.concatenate([jnp.where(even, mine, theirs), jnp.where(even, theirs, mine)], axis=2)
    later = by_core(rows[1], ("z", 1), ("z", 3))
    sooner = by_core(rows[0], ("z", 0), ("z", 2))
    rows = jnp.concatenate([jnp.concatenate([sooner, later], axis=0), stat], axis=1)
    rows1, rows3 = across(rows, 1), across(rows, 3)
    rows2 = jnp.concatenate([across(rows1[0:CAP], 1), across(rows3[CAP : 2 * CAP], 3)], axis=0)
    stat = coded(summed(*[part[:, 1024:1152] for part in (rows, rows1, rows2, rows3)]))
    early = jnp.stack([part[:, 0:1024] for part in (rows, rows1, rows3)])
    late = rows2[None, :, 0:1024]
    early1, early3 = along(early, 1), along(early, 3)
    late1, late3 = along(late, 1), along(late, 3)
    early2 = along(early1[0:2], 1), along(early3[2:3], 3)
    late2 = along(late3, 3)
    mine = jnp.concatenate(
        [
            early[0:2], late, early[2:3], early1[0:2], late1, early1[2:3],
            early2[0], late2, early2[1], early3[0:2], late3, early3[2:3],
        ],
        axis=0,
    )
    theirs = move(mine, "core", 1)
    gate, up, down = gate_weight[0], up_weight[0], down_weight[0]
    block = shape((4, 96, 1024), BF)

    mine = call(
        ffn_own,
        [block] * 4,
        [SMEM] + [VMEM] * 5,
        30,
        [pltpu.VMEM((384, 384), BF)],
        flops=6 * 384 * 2048 * 768,
        moved=12 * 10**6,
        name="experts_own",
    )(here, mine, inverse, gate, up, down)
    act, theirs2 = call(
        ffn_other,
        [shape((384, 384), BF), block],
        [SMEM] + [VMEM] * 6,
        28,
        flops=5 * 384 * 2048 * 768,
        moved=10 * 10**6,
        name="experts_other",
    )(here, theirs, inverse, gate, up, down, mine[0])
    theirs = call(
        ffn_rest,
        [block] * 3,
        [SMEM] + [VMEM] * 2,
        20,
        flops=384 * 3072 * 768,
        moved=5 * 10**6,
        name="experts_rest",
    )(here, act, down)
    part2 = add(mine[2], move(theirs2, "core", 1))
    far1, far3 = along(part2[0:2], 1), along(part2[2:4], 3)
    part1 = add(mine[1], move(theirs[1], "core", 1))
    part3 = add(mine[3], move(theirs[2], "core", 1))
    part0 = add(mine[0], move(theirs[0], "core", 1))
    near1, near3 = along(part1[2:4], 1), along(part3[0:2], 3)
    next1, next3 = along(add(part1[0:2], far1), 1), along(add(part3[2:4], far3), 3)
    lines = jnp.concatenate(
        [add(part0[0:2], next1, near3), add(part0[2:4], near1, next3)], axis=0
    )
    lines = add(lines[0], *[across(lines[k], k) for k in (1, 2, 3)])
    later = by_core(lines[CAP : 2 * CAP], ("z", 3), ("z", 1))
    sooner = by_core(lines[0:CAP], ("z", 0), ("z", 2))
    lines = jnp.stack([sooner, later])
    left, right = lines[:, :, 0:512], lines[:, :, 512:1024]
    mine = jnp.where(even, left, right)
    theirs = jnp.concatenate([jnp.where(even, right, left), stat.reshape(2, CAP, 128)], axis=2)
    theirs = move(theirs, "core", 1)
    stat = jnp.where(even, stat, theirs[:, :, 512:640].reshape(2 * CAP, 128))
    theirs = theirs[:, :, 0:512]
    out = call(
        final_kernel,
        shape((ROWS, 512), BF),
        [SMEM] + [VMEM] * 5,
        8,
        flops=10**8,
        moved=10**6,
        name="combine",
    )(here, mine, theirs, stat, hidden, named)
    new_conv = new_conv.transpose(1, 0, 2)
    return (out, new_state, new_conv)


def solution(mesh):
    grid = Mesh(mesh.devices.reshape(4, 4, 4, 2), AXES)
    group, tensor = ("z", "y"), ("x", "core")
    return jax.shard_map(
        per_device,
        mesh=grid,
        in_specs=(
            P(group, tensor),
            P(group, tensor),
            P(group, None, tensor),
            P(group, None, tensor),
            P(group, None),
            P(group, None),
            P(group, None),
            P(None, tensor),
            P(tensor),
            P(tensor, None),
            P(tensor, None),
            P(),
            P(None, tensor),
            P(tensor),
            P(None, tensor),
            P(tensor),
            P(tensor, None),
            P(group, tensor),
            P(tensor),
            P(tensor, None),
            P(group, None),
            P(group, None, tensor),
            P(group, None, tensor),
            P(group, tensor, None),
        ),
        out_specs=(P(group, tensor), P(group, None, tensor), P(group, None, tensor)),
        check_vma=False,
    )
```

```python
import functools

import jax
import jax.numpy as jnp
import numpy as np
from jax import lax
from jax.experimental import pallas as pl
from jax.experimental.pallas import tpu as pltpu
from jax.sharding import Mesh
from jax.sharding import PartitionSpec as P

DEC = 16
ROWS = 64
SEQ = 20
CAP = 48
NS = 16
TAPS = 4
EXPERTS = 4
EPS = 1e-6
BF = jnp.bfloat16
F32 = jnp.float32
I32 = jnp.int32
VMEM = pl.BlockSpec(memory_space=pltpu.VMEM)
SMEM = pl.BlockSpec(memory_space=pltpu.SMEM)
HBM = pl.BlockSpec(memory_space=pltpu.HBM)
AXES = ("z", "y", "x", "core")


def params(mib):
    return pltpu.CompilerParams(vmem_limit_bytes=mib * 1024 * 1024)


def iota(shape, dim):
    return lax.broadcasted_iota(I32, shape, dim)


def silu(v):
    return v / (1.0 + jnp.exp(-v))


def dot(a, b):
    return jnp.dot(a, b, preferred_element_type=F32)


def span_starts(span_ref):
    s1 = DEC + span_ref[0, 0]
    s2 = s1 + span_ref[0, 1]
    s3 = s2 + span_ref[0, 2]
    return (jnp.int32(DEC), s1, s2, s3)


def conv_kernel(
    span_hbm, res_hbm, slot_hbm, x_hbm, cache_hbm, w_hbm, b_hbm, rank_hbm, sw_hbm, gain_hbm,
    cx_ref, proj_ref,
    span_ref, res_ref, slot_ref, x_ref, cache_ref, w_ref, b_ref, rank_ref, sw_ref, gain_ref, sems,
):
    sources = (span_hbm, res_hbm, slot_hbm, x_hbm, cache_hbm, w_hbm, b_hbm, gain_hbm, sw_hbm, rank_hbm)
    targets = (span_ref, res_ref, slot_ref, x_ref, cache_ref, w_ref, b_ref, gain_ref, sw_ref, rank_ref)
    copies = [
        pltpu.make_async_copy(source, target, sems.at[i])
        for i, (source, target) in enumerate(zip(sources, targets))
    ]
    for copy in copies:
        copy.start()
    for copy in copies[:7]:
        copy.wait()
    starts = span_starts(span_ref)
    x = x_ref[...]
    r = iota((ROWS, 128), 0)
    j = iota((ROWS, 128), 1)
    start = jnp.where(r < DEC, r, DEC)
    slot = jnp.full((ROWS, 128), slot_ref[0, DEC], I32)
    res = jnp.full((ROWS, 128), res_ref[0, 0], I32)
    for c in range(1, 4):
        inside = r >= starts[c]
        start = jnp.where(inside, starts[c], start)
        slot = jnp.where(inside, slot_ref[0, DEC + c], slot)
        res = jnp.where(inside, res_ref[0, c], res)
    for d in range(DEC):
        slot = jnp.where(r == d, slot_ref[0, d], slot)
    res = jnp.where(r < DEC, 1, res)
    pos = r - start

    def select(column, line, width):
        return (j == jnp.where(line, column, -1)).astype(F32)[:, 0:width].astype(BF)

    total = b_ref[...] + w_ref[TAPS - 1 : TAPS] * x.astype(F32)
    for lag in range(1, TAPS):
        value = dot(select(r - lag, pos >= lag, ROWS), x)
        for i in range(TAPS - 1):
            old = (pos == i + lag - 3) & (pos < lag) & (res > 0)
            value = value + dot(select(slot, old, SEQ), cache_ref[i])
        total = total + w_ref[TAPS - 1 - lag : TAPS - lag] * value
    cx = silu(total).astype(BF)
    cx_ref[...] = cx
    for copy in copies[7:]:
        copy.wait()
    proj_ref[0:ROWS, 0:512] = dot(cx, rank_ref[...]).astype(BF)
    proj_ref[0:ROWS, 512:640] = jnp.zeros((ROWS, 128), BF)
    proj_ref[0:ROWS, 512 : 512 + 2 * NS] = lax.dot_general(
        cx, sw_ref[...], (((1,), (1,)), ((), ())), preferred_element_type=F32
    ).astype(BF)
    line = 2 * (2 * lax.axis_index("x") + lax.axis_index("core"))
    inverse = 1.0 / (gain_ref[...] * gain_ref[...])
    high = inverse.astype(BF).astype(F32)
    row = iota((16, 512), 0)
    extra = jnp.where(row == line, high, jnp.where(row == line + 1, inverse - high, 0.0))
    proj_ref[ROWS : ROWS + 16, 0:512] = extra.astype(BF)
    proj_ref[ROWS : ROWS + 16, 512:640] = jnp.zeros((16, 128), BF)


def tail_kernel(span_ref, res_ref, slot_ref, x_ref, cache_ref, nc_ref):
    starts = span_starts(span_ref)
    x = x_ref[...]
    group = iota((SEQ, 128), 0)
    j = iota((SEQ, 128), 1)
    length = jnp.ones((SEQ, 128), I32)
    first = jnp.zeros((SEQ, 128), I32)
    kept = jnp.ones((SEQ, 128), I32)
    for s in range(SEQ):
        here = group == slot_ref[0, s]
        if s < DEC:
            first = jnp.where(here, s, first)
        else:
            first = jnp.where(here, starts[s - DEC], first)
            length = jnp.where(here, span_ref[0, s - DEC], length)
            kept = jnp.where(here, res_ref[0, s - DEC], kept)

    def select(column, line, width):
        return (j == jnp.where(line, column, -1)).astype(F32)[:, 0:width].astype(BF)

    for offset in range(TAPS - 1):
        back = length - (TAPS - 1) + offset
        value = dot(select(first + back, back >= 0, ROWS), x)
        for i in range(TAPS - 1):
            old = (back == i - 3) & (kept > 0)
            value = value + dot(select(group, old, SEQ), cache_ref[i])
        nc_ref[offset] = value.astype(BF)


def scan_kernel(
    here_ref, span_ref, res_ref, slot_ref,
    q0_ref, q1_ref, q2_ref, q3_ref, cx_ref, z_ref, gain_ref, sw_ref, sb_ref, dl_ref, skip_ref,
    sc_ref, ow_ref,
    ns_ref, own_ref, sib_ref, inv_ref,
    state_ref, w_vmem, step_ref, drive_ref, bb_ref, cb_ref, pc_ref, tr_ref, sem, state_sem,
):
    fetch = pltpu.make_async_copy(ow_ref, w_vmem, sem)
    fetch.start()
    starts = span_starts(span_ref)
    sums = (
        q0_ref[...].astype(F32) + q1_ref[...].astype(F32)
        + q2_ref[...].astype(F32) + q3_ref[...].astype(F32)
    )
    proj = sums[0:ROWS]
    for t in range(8):
        inverse = sums[ROWS + 2 * t : ROWS + 2 * t + 1, 0:512] + sums[ROWS + 2 * t + 1 : ROWS + 2 * t + 2, 0:512]
        inv_ref[t // 2, :, 512 * (t % 2) : 512 * (t % 2) + 512] = inverse
    low = proj[:, 0:512]
    mean = jnp.mean(low * low, axis=1, keepdims=True)
    norm = (low * lax.rsqrt(mean + EPS) * gain_ref[...]).astype(BF)
    pre = dot(norm, sw_ref[...]) + sb_ref[...]
    step = jnp.maximum(pre, 0.0) + jnp.log1p(jnp.exp(-jnp.abs(pre)))
    values = cx_ref[...].astype(F32)
    step_ref[...] = step
    drive_ref[...] = step * values
    tr_ref[0:ROWS] = proj[:, 512:640]
    tr_ref[ROWS : 2 * ROWS] = jnp.zeros((ROWS, 128), F32)
    turned = tr_ref[...].T
    for r in range(ROWS):
        bb_ref[r] = jnp.broadcast_to(turned[0:NS, r : r + 1], (NS, 128))
        cb_ref[r] = jnp.broadcast_to(turned[NS : 2 * NS, r : r + 1], (NS, 128))
    rate = -jnp.exp(dl_ref[...])
    groups = rate.shape[1] // 128

    def advance(r, state):
        c1 = (r >= starts[1]).astype(I32)
        c2 = (r >= starts[2]).astype(I32)
        c3 = (r >= starts[3]).astype(I32)
        piece = c1 + c2 + c3
        decode = r < DEC
        slot = slot_ref[0, jnp.where(decode, r, DEC + piece)]
        resumed = jnp.where(decode, 1, res_ref[0, piece])
        begins = (r <= DEC) | (r == starts[1]) | (r == starts[2]) | (r == starts[3])
        keep = jnp.where(begins, 0.0, 1.0).astype(F32)
        load = jnp.where(begins, resumed, 0).astype(F32)
        prior = state * keep + sc_ref[slot] * load
        decay = jnp.exp(step_ref[pl.ds(r, 1), :] * rate)
        b = jnp.concatenate([bb_ref[r]] * groups, axis=1)
        c = jnp.concatenate([cb_ref[r]] * groups, axis=1)
        fresh = decay * prior + drive_ref[pl.ds(r, 1), :] * b
        weighed = fresh * c
        pc_ref[r] = weighed[0:8] + weighed[8:16]
        state_ref[slot] = fresh
        return fresh

    lax.fori_loop(0, ROWS, advance, jnp.zeros(rate.shape, F32), unroll=4)
    keep = pltpu.make_async_copy(state_ref, ns_ref, state_sem)
    keep.start()
    output = skip_ref[...] * values
    for k in range(8):
        output = output + pc_ref[:, k, :]
    gated = (output * silu(z_ref[...].astype(F32))).astype(BF)
    fetch.wait()
    x, c = here_ref[0], here_ref[1]
    for out, core in ((own_ref, c), (sib_ref, 1 - c)):
        for k in range(4):
            cols = pl.ds(pl.multiple_of((2 * lax.rem(x + k, 4) + core) * 512, 512), 512)
            out[k] = dot(gated, w_vmem[:, cols]).astype(BF)
    keep.wait()


def pick_kernel(
    here_ref, q0_ref, q1_ref, q2_ref, q3_ref, resid_ref, gain_ref, router_ref, chosen_ref,
    hid_ref, mine_ref, theirs_ref, named_ref,
):
    mixer = (
        q0_ref[...].astype(F32) + q1_ref[...].astype(F32)
        + q2_ref[...].astype(F32) + q3_ref[...].astype(F32)
    ).astype(BF)
    hidden = resid_ref[...].astype(F32) + mixer.astype(F32)
    hid_ref[...] = hidden
    scaled = (hidden * gain_ref[...]).astype(BF)
    wide = scaled.astype(F32)
    lane = iota((ROWS, 128), 1)
    squares = jnp.sum(hidden * hidden, axis=1, keepdims=True)
    stat = jnp.where(lane % 64 == EXPERTS, squares, 0.0)
    for e in range(EXPERTS):
        part = jnp.sum(wide * router_ref[e : e + 1].astype(F32), axis=1, keepdims=True)
        stat = jnp.where(lane % 64 == e, part, stat)
    high = stat.astype(BF).astype(F32)
    stat = jnp.where(lane < 64, high, stat - high).astype(BF)
    for out in (mine_ref, theirs_ref):
        out[0, :, 512:640] = stat[0:CAP]
        out[1, :, 512:640] = jnp.concatenate([stat[CAP:ROWS], jnp.zeros((2 * CAP - ROWS, 128), BF)], axis=0)
    before = (iota((ROWS, ROWS), 0) < iota((ROWS, ROWS), 1)).astype(F32).astype(BF)
    row = iota((CAP, ROWS), 0)
    z, core = here_ref[2], here_ref[1]
    expert = lax.rem(z + 2 * core + iota((8, ROWS), 0), EXPERTS)
    marks = ((chosen_ref[0:1] == expert) | (chosen_ref[1:2] == expert)).astype(F32)
    place = dot(marks.astype(BF), before)
    place = jnp.where(marks > 0.0, place, -1.0).astype(I32)
    for i in range(4):
        hot = (row == place[i : i + 1]).astype(F32).astype(BF)
        out = mine_ref if i < 2 else theirs_ref
        out[i % 2, :, 0:512] = dot(hot, scaled).astype(BF)
    same = (iota((ROWS, ROWS), 0) == iota((ROWS, ROWS), 1)).astype(F32).astype(BF)
    pair = iota((8, ROWS), 0)
    both = jnp.where(pair == 0, chosen_ref[0:1], jnp.where(pair == 1, chosen_ref[1:2], 0))
    turned = lax.dot_general(
        same, both.astype(F32).astype(BF), (((1,), (1,)), ((), ())), preferred_element_type=F32
    )
    named_ref[...] = jnp.zeros_like(named_ref)
    named_ref[:, 0:8] = turned.astype(I32)


def experts_in(here_ref, side, x_ref, inv_ref, wg_ref, wu_ref):
    x = here_ref[0]
    place = (0, 1, 3, 2)
    both = square = None
    for k in range(4):
        there = lax.rem(x + 4 - k, 4)
        rows = pl.ds(pl.multiple_of(there * 1024, 1024), 1024)
        block = jnp.concatenate(
            [x_ref[jnp.where(side == 0, 4 * place[j] + k, 4 * place[k] + j)] for j in range(4)], axis=0
        )
        part = dot(block, jnp.concatenate([wg_ref[rows, :], wu_ref[rows, :]], axis=1))
        wide = block.astype(F32)
        wide = wide * wide * inv_ref[there]
        square_part = wide[:, 0:128]
        for lane in range(128, 1024, 128):
            square_part = square_part + wide[:, lane : lane + 128]
        if k == 0:
            both, square = part, square_part
        else:
            both, square = both + part, square + square_part
    both = both * lax.rsqrt(jnp.sum(square, axis=1, keepdims=True) / 4096.0 + EPS)
    return (silu(both[:, 0:384]) * both[:, 384:768]).astype(BF)


def experts_out(here_ref, side, act_ref, wd_ref, outs):
    x = here_ref[0]

    def product(rows, there):
        cols = pl.ds(pl.multiple_of(there * 1024, 1024), 1024)
        return dot(rows, wd_ref[:, cols]).astype(BF)

    @pl.when(side == 0)
    def _():
        owners = [j for j in range(4) if (4 - j) % 4 in outs]
        rows = jnp.concatenate([act_ref[96 * j : 96 * j + 96, :] for j in owners], axis=0)
        for n in range(4):
            value = product(rows, lax.rem(x + n, 4))
            for i, j in enumerate(owners):
                outs[(4 - j) % 4][n] = value[96 * i : 96 * i + 96]

    @pl.when(side == 1)
    def _():
        for m in outs:
            value = product(act_ref[...], lax.rem(x + m, 4))
            for j in range(4):
                outs[m][(4 - j) % 4] = value[96 * j : 96 * j + 96]


def gather_in(here_ref, terms, inv_ref, wg_ref, wu_ref):
    both = square = None
    for k, blocks in terms:
        there = lax.rem(here_ref[0] + 4 - k, 4)
        rows = pl.ds(pl.multiple_of(there * 1024, 1024), 1024)
        block = jnp.concatenate(blocks, axis=0)
        part = dot(block, jnp.concatenate([wg_ref[rows, :], wu_ref[rows, :]], axis=1))
        wide = block.astype(F32)
        wide = wide * wide * inv_ref[there]
        square_part = wide[:, 0:128]
        for lane in range(128, 1024, 128):
            square_part = square_part + wide[:, lane : lane + 128]
        if both is None:
            both, square = part, square_part
        else:
            both, square = both + part, square + square_part
    return both, square


def activate(both, square):
    both = both * lax.rsqrt(jnp.sum(square, axis=1, keepdims=True) / 4096.0 + EPS)
    return (silu(both[:, 0:384]) * both[:, 384:768]).astype(BF)


def ffn_early(here_ref, x_ref, inv_ref, wg_ref, wu_ref, wd_ref, acc_ref, sq_ref):
    weights = (inv_ref, wg_ref, wu_ref)

    @pl.when(here_ref[1] == 0)
    def _():
        terms = [(k, [x_ref[4 * i + k] for i in range(3)]) for k in range(4)]
        both, square = gather_in(here_ref, terms, *weights)
        for out, value in ((acc_ref, both), (sq_ref, square)):
            out[0:192] = value[0:192]
            out[192:288] = jnp.zeros_like(value[0:96])
            out[288:384] = value[192:288]

    @pl.when(here_ref[1] == 1)
    def _():
        terms = [(k, [x_ref[4 * i + n] for n in range(4)]) for i, k in enumerate((0, 1, 3))]
        acc_ref[...], sq_ref[...] = gather_in(here_ref, terms, *weights)


def ffn_late(here_ref, x_ref, inv_ref, wg_ref, wu_ref, acc_ref, sq_ref, act_ref):
    weights = (inv_ref, wg_ref, wu_ref)

    @pl.when(here_ref[1] == 0)
    def _():
        terms = [(k, [x_ref[k]]) for k in range(4)]
        both, square = gather_in(here_ref, terms, *weights)
        act_ref[0:192] = activate(acc_ref[0:192], sq_ref[0:192])
        act_ref[192:288] = activate(both, square)
        act_ref[288:384] = activate(acc_ref[288:384], sq_ref[288:384])

    @pl.when(here_ref[1] == 1)
    def _():
        both, square = gather_in(here_ref, [(2, [x_ref[n] for n in range(4)])], *weights)
        act_ref[...] = activate(acc_ref[...] + both, sq_ref[...] + square)


def ffn_own(here_ref, act_ref, wd_ref, p0_ref, p1_ref, p2_ref, p3_ref):
    experts_out(here_ref, here_ref[1], act_ref, wd_ref, {0: p0_ref, 1: p1_ref, 2: p2_ref, 3: p3_ref})


def ffn_other(
    here_ref, x_ref, inv_ref, wg_ref, wu_ref, wd_ref, earlier_ref,
    p0_ref, p1_ref, p2_ref, p3_ref, act_ref,
):
    side = 1 - here_ref[1]
    act_ref[...] = experts_in(here_ref, side, x_ref, inv_ref, wg_ref, wu_ref)
    experts_out(here_ref, side, act_ref, wd_ref, {0: p0_ref, 1: p1_ref, 2: p2_ref, 3: p3_ref})


def final_kernel(
    here_ref, mine_ref, theirs_ref, stat_ref, hid_ref, chosen_ref, out_ref,
):
    stat = stat_ref[0:ROWS].astype(F32)

    def column(e):
        return stat[:, e : e + 1] + stat[:, 64 + e : 65 + e]

    scale = lax.rsqrt(column(EXPERTS) / 4096.0 + EPS)
    e0, e1 = chosen_ref[:, 0:1], chosen_ref[:, 1:2]
    l0 = jnp.zeros((ROWS, 1), F32)
    l1 = jnp.zeros((ROWS, 1), F32)
    for e in range(EXPERTS):
        l0 = l0 + jnp.where(e0 == e, column(e), 0.0)
        l1 = l1 + jnp.where(e1 == e, column(e), 0.0)
    gap = (l0 - l1) * scale
    route0 = 1.0 / (1.0 + jnp.exp(-gap))
    route1 = 1.0 / (1.0 + jnp.exp(gap))
    before = (iota((ROWS, ROWS), 1) < iota((ROWS, ROWS), 0)).astype(F32).astype(BF)
    lane = iota((ROWS, CAP), 1)
    total = hid_ref[...]
    z, core = here_ref[2], here_ref[1]
    expert = lax.rem(z + 2 * core + iota((ROWS, 128), 1), EXPERTS)
    first, second = e0 == expert, e1 == expert
    marks = (first | second).astype(F32)
    place = dot(before, marks.astype(BF))
    place = jnp.where(marks > 0.0, place, -1.0).astype(I32)
    weight = jnp.where(first, route0, jnp.where(second, route1, 0.0))
    for i in range(4):
        hot = (lane == place[:, i : i + 1]).astype(F32).astype(BF)
        ref = mine_ref if i < 2 else theirs_ref
        total = total + weight[:, i : i + 1] * dot(hot, ref[i % 2])
    out_ref[...] = total.astype(BF)


def move(value, axis, shift):
    size = lax.axis_size(axis)
    return lax.ppermute(value, axis, [(i, (i + shift) % size) for i in range(size)])


def by_core(value, first, second):
    sizes = tuple(lax.axis_size(name) for name in AXES)
    pairs = []
    for source in range(int(np.prod(sizes))):
        place = list(np.unravel_index(source, sizes))
        axis, shift = (first, second)[int(place[3])]
        at = AXES.index(axis)
        place[at] = (place[at] + shift) % sizes[at]
        pairs.append((source, int(np.ravel_multi_index(place, sizes))))
    return lax.ppermute(value, AXES, pairs)


def across(value, shift):
    return by_core(value, ("x", shift), ("y", shift))


def along(value, shift):
    return by_core(value, ("y", shift), ("x", shift))


def summed(*values):
    total = values[0].astype(F32)
    for value in values[1:]:
        total = total + value.astype(F32)
    return total[..., 0:64] + total[..., 64:128]


def coded(value):
    high = value.astype(BF)
    low = (value - high.astype(F32)).astype(BF)
    return jnp.concatenate([high, low], axis=-1)


def add(*values):
    total = values[0].astype(F32)
    for value in values[1:]:
        total = total + value.astype(F32)
    return total.astype(BF)


def stay(value):
    return pltpu.with_memory_space_constraint(value, pltpu.HBM)


def call(kernel, outs, ins, mib, scratch=(), flops=0, moved=0, name=None, out_specs=None):
    single = not isinstance(outs, (list, tuple))
    return pl.pallas_call(
        kernel,
        out_shape=outs,
        in_specs=ins,
        out_specs=out_specs or (VMEM if single else [VMEM] * len(outs)),
        scratch_shapes=list(scratch),
        compiler_params=params(mib),
        cost_estimate=pl.CostEstimate(flops=flops, bytes_accessed=moved, transcendentals=0),
        name=name,
    )


def shape(dims, dtype):
    return jax.ShapeDtypeStruct(dims, dtype)


def per_device(
    conv_input, gate_input, conv_cache, state_cache, span_lengths, span_resumes, slot_index,
    conv_weight, conv_bias, rank_weight, state_weight, step_gain, step_weight, step_bias,
    decay_log, skip_gain, out_weight, residual, moe_gain, router_weight, chosen_experts,
    gate_weight, up_weight, down_weight,
):
    here = jnp.stack(
        [lax.axis_index("x"), lax.axis_index("core"), lax.axis_index("z")]
    ).astype(I32)
    even = lax.axis_index("core") == 0
    old = conv_cache.transpose(1, 0, 2)
    cx, proj = call(
        conv_kernel,
        [shape((ROWS, 1024), BF), shape((ROWS + 16, 640), BF)],
        [HBM] * 10,
        16,
        [
            pltpu.SMEM((1, 4), I32),
            pltpu.SMEM((1, 4), I32),
            pltpu.SMEM((1, SEQ), I32),
            pltpu.VMEM((ROWS, 1024), BF),
            pltpu.VMEM((3, SEQ, 1024), BF),
            pltpu.VMEM((TAPS, 1024), F32),
            pltpu.VMEM((1, 1024), F32),
            pltpu.VMEM((1024, 512), BF),
            pltpu.VMEM((2 * NS, 1024), BF),
            pltpu.VMEM((1, 512), F32),
            pltpu.SemaphoreType.DMA((10,)),
        ],
        flops=10**9,
        moved=2 * 10**6,
        name="conv",
    )(
        *map(
            stay,
            (
                span_lengths, span_resumes, slot_index, conv_input,
                old, conv_weight, conv_bias.reshape(1, 1024),
                rank_weight, state_weight.T, moe_gain.reshape(1, 512),
            ),
        )
    )
    new_conv = call(
        tail_kernel,
        shape((3, SEQ, 1024), BF),
        [SMEM] * 3 + [VMEM] * 2,
        8,
        flops=10**9,
        moved=10**6,
        name="tail",
    )(span_lengths, span_resumes, slot_index, conv_input, old)
    chip = add(proj, move(proj, "core", 1))
    parts = [chip] + [move(chip, "x", k) for k in (1, 2, 3)]
    new_state, own, sib, inverse = call(
        scan_kernel,
        [
            shape((SEQ, NS, 1024), F32),
            shape((4, ROWS, 512), BF),
            shape((4, ROWS, 512), BF),
            shape((4, 1, 1024), F32),
        ],
        [SMEM] * 4 + [VMEM] * 12 + [HBM],
        32,
        [
            pltpu.VMEM((SEQ, NS, 1024), F32),
            pltpu.VMEM((1024, 4096), BF),
            pltpu.VMEM((ROWS, 1024), F32),
            pltpu.VMEM((ROWS, 1024), F32),
            pltpu.VMEM((ROWS, NS, 128), F32),
            pltpu.VMEM((ROWS, NS, 128), F32),
            pltpu.VMEM((ROWS, 8, 1024), F32),
            pltpu.VMEM((128, 128), F32),
            pltpu.SemaphoreType.DMA,
            pltpu.SemaphoreType.DMA,
        ],
        flops=10**9,
        moved=10**7,
        name="scan",
        out_specs=[HBM] + [VMEM] * 3,
    )(
        here, span_lengths, span_resumes, slot_index, *parts, cx, gate_input,
        step_gain.reshape(1, 512), step_weight, step_bias.reshape(1, 1024), decay_log,
        skip_gain.reshape(1, 1024), state_cache, stay(out_weight),
    )
    mixed = add(own, move(sib, "core", 1))
    parts = [mixed[0]] + [move(mixed[k], "x", k) for k in (1, 2, 3)]
    hidden, mine, theirs, named = call(
        pick_kernel,
        [
            shape((ROWS, 512), F32),
            shape((2, CAP, 640), BF),
            shape((2, CAP, 640), BF),
            shape((ROWS, 128), I32),
        ],
        [SMEM] + [VMEM] * 8,
        8,
        flops=10**8,
        moved=10**6,
        name="pick",
    )(here, *parts, residual, moe_gain.reshape(1, 512), router_weight.T, chosen_experts.T)
    theirs = move(theirs, "core", 1)
    stat = coded(summed(mine[:, :, 512:640], theirs[:, :, 512:640])).reshape(2 * CAP, 128)
    mine, theirs = mine[:, :, 0:512], theirs[:, :, 0:512]
    rows = jnp.concatenate([jnp.where(even, mine, theirs), jnp.where(even, theirs, mine)], axis=2)
    later = by_core(rows[1], ("z", 1), ("z", 3))
    sooner = by_core(rows[0], ("z", 0), ("z", 2))
    rows = jnp.concatenate([jnp.concatenate([sooner, later], axis=0), stat], axis=1)
    rows1, rows3 = across(rows, 1), across(rows, 3)
    rows2 = jnp.concatenate([across(rows1[0:CAP], 1), across(rows3[CAP : 2 * CAP], 3)], axis=0)
    stat = coded(summed(*[part[:, 1024:1152] for part in (rows, rows1, rows2, rows3)]))
    early = jnp.stack([part[:, 0:1024] for part in (rows, rows1, rows3)])
    late = rows2[None, :, 0:1024]
    early1, early3 = along(early, 1), along(early, 3)
    late1, late3 = along(late, 1), along(late, 3)
    early2 = along(early1[0:2], 1), along(early3[2:3], 3)
    late2 = along(late3, 3)
    most = jnp.concatenate(
        [
            early[0:2], late, early[2:3], early1[0:2], late1, early1[2:3],
            early3[0:2], late3, early3[2:3],
        ],
        axis=0,
    )
    last = jnp.concatenate([early2[0], late2, early2[1]], axis=0)
    their_most = move(most, "core", 1)
    gate, up, down = gate_weight[0], up_weight[0], down_weight[0]
    block = shape((4, 96, 1024), BF)

    acc, square = call(
        ffn_early,
        [shape((384, 768), F32), shape((384, 128), F32)],
        [SMEM] + [VMEM] * 5,
        20,
        flops=2 * 288 * 4096 * 768,
        moved=8 * 10**6,
        name="experts_early",
    )(here, most, inverse, gate, up, down)
    last, acc = lax.optimization_barrier((last, acc))
    their_last = move(last, "core", 1)
    own = call(
        ffn_late,
        shape((384, 384), BF),
        [SMEM] + [VMEM] * 6,
        16,
        flops=2 * 96 * 4096 * 768,
        moved=8 * 10**6,
        name="experts_late",
    )(here, last, inverse, gate, up, acc, square)
    theirs = jnp.concatenate([their_most, their_last], axis=0)
    theirs = call(
        ffn_other,
        [block] * 4,
        [SMEM] + [VMEM] * 6,
        24,
        [pltpu.VMEM((384, 384), BF)],
        flops=6 * 384 * 2048 * 768,
        moved=10 * 10**6,
        name="experts_other",
    )(here, theirs, inverse, gate, up, down, own)
    mine = call(
        ffn_own,
        [block] * 4,
        [SMEM] + [VMEM] * 2,
        13,
        flops=384 * 4096 * 768,
        moved=5 * 10**6,
        name="experts_own",
    )(here, own, down)
    part2 = add(mine[2], move(theirs[2], "core", 1))
    far1, far3 = along(part2[0:2], 1), along(part2[2:4], 3)
    part1 = add(mine[1], move(theirs[1], "core", 1))
    part3 = add(mine[3], move(theirs[3], "core", 1))
    part0 = add(mine[0], move(theirs[0], "core", 1))
    near1, near3 = along(part1[2:4], 1), along(part3[0:2], 3)
    next1, next3 = along(add(part1[0:2], far1), 1), along(add(part3[2:4], far3), 3)
    lines = jnp.concatenate(
        [add(part0[0:2], next1, near3), add(part0[2:4], near1, next3)], axis=0
    )
    lines = add(lines[0], *[across(lines[k], k) for k in (1, 2, 3)])
    later = by_core(lines[CAP : 2 * CAP], ("z", 3), ("z", 1))
    sooner = by_core(lines[0:CAP], ("z", 0), ("z", 2))
    lines = jnp.stack([sooner, later])
    left, right = lines[:, :, 0:512], lines[:, :, 512:1024]
    mine = jnp.where(even, left, right)
    theirs = jnp.concatenate([jnp.where(even, right, left), stat.reshape(2, CAP, 128)], axis=2)
    theirs = move(theirs, "core", 1)
    stat = jnp.where(even, stat, theirs[:, :, 512:640].reshape(2 * CAP, 128))
    theirs = theirs[:, :, 0:512]
    out = call(
        final_kernel,
        shape((ROWS, 512), BF),
        [SMEM] + [VMEM] * 5,
        8,
        flops=10**8,
        moved=10**6,
        name="combine",
    )(here, mine, theirs, stat, hidden, named)
    new_conv = new_conv.transpose(1, 0, 2)
    return (out, new_state, new_conv)


def solution(mesh):
    grid = Mesh(mesh.devices.reshape(4, 4, 4, 2), AXES)
    group, tensor = ("z", "y"), ("x", "core")
    return jax.shard_map(
        per_device,
        mesh=grid,
        in_specs=(
            P(group, tensor),
            P(group, tensor),
            P(group, None, tensor),
            P(group, None, tensor),
            P(group, None),
            P(group, None),
            P(group, None),
            P(None, tensor),
            P(tensor),
            P(tensor, None),
            P(tensor, None),
            P(),
            P(None, tensor),
            P(tensor),
            P(None, tensor),
            P(tensor),
            P(tensor, None),
            P(group, tensor),
            P(tensor),
            P(tensor, None),
            P(group, None),
            P(group, None, tensor),
            P(group, None, tensor),
            P(group, tensor, None),
        ),
        out_specs=(P(group, tensor), P(group, None, tensor), P(group, None, tensor)),
        check_vma=False,
    )
```

```python
import functools

import jax
import jax.numpy as jnp
import numpy as np
from jax import lax
from jax.experimental import pallas as pl
from jax.experimental.pallas import tpu as pltpu
from jax.sharding import Mesh
from jax.sharding import PartitionSpec as P

DEC = 16
ROWS = 64
SEQ = 20
CAP = 48
NS = 16
TAPS = 4
EXPERTS = 4
EPS = 1e-6
BF = jnp.bfloat16
F32 = jnp.float32
I32 = jnp.int32
VMEM = pl.BlockSpec(memory_space=pltpu.VMEM)
SMEM = pl.BlockSpec(memory_space=pltpu.SMEM)
HBM = pl.BlockSpec(memory_space=pltpu.HBM)
AXES = ("z", "y", "x", "core")


def params(mib):
    return pltpu.CompilerParams(vmem_limit_bytes=mib * 1024 * 1024)


def iota(shape, dim):
    return lax.broadcasted_iota(I32, shape, dim)


def silu(v):
    return v / (1.0 + jnp.exp(-v))


def dot(a, b):
    return jnp.dot(a, b, preferred_element_type=F32)


def span_starts(span_ref):
    s1 = DEC + span_ref[0, 0]
    s2 = s1 + span_ref[0, 1]
    s3 = s2 + span_ref[0, 2]
    return (jnp.int32(DEC), s1, s2, s3)


def conv_kernel(
    span_hbm, res_hbm, slot_hbm, x_hbm, cache_hbm, w_hbm, b_hbm, rank_hbm, sw_hbm, gain_hbm,
    cx_ref, proj_ref,
    span_ref, res_ref, slot_ref, x_ref, cache_ref, w_ref, b_ref, rank_ref, sw_ref, gain_ref, sems,
):
    sources = (span_hbm, res_hbm, slot_hbm, x_hbm, cache_hbm, w_hbm, b_hbm, gain_hbm, sw_hbm, rank_hbm)
    targets = (span_ref, res_ref, slot_ref, x_ref, cache_ref, w_ref, b_ref, gain_ref, sw_ref, rank_ref)
    copies = [
        pltpu.make_async_copy(source, target, sems.at[i])
        for i, (source, target) in enumerate(zip(sources, targets))
    ]
    for copy in copies:
        copy.start()
    for copy in copies[:7]:
        copy.wait()
    starts = span_starts(span_ref)
    x = x_ref[...]
    r = iota((ROWS, 128), 0)
    j = iota((ROWS, 128), 1)
    start = jnp.where(r < DEC, r, DEC)
    slot = jnp.full((ROWS, 128), slot_ref[0, DEC], I32)
    res = jnp.full((ROWS, 128), res_ref[0, 0], I32)
    for c in range(1, 4):
        inside = r >= starts[c]
        start = jnp.where(inside, starts[c], start)
        slot = jnp.where(inside, slot_ref[0, DEC + c], slot)
        res = jnp.where(inside, res_ref[0, c], res)
    for d in range(DEC):
        slot = jnp.where(r == d, slot_ref[0, d], slot)
    res = jnp.where(r < DEC, 1, res)
    pos = r - start

    def select(column, line, width):
        return (j == jnp.where(line, column, -1)).astype(F32)[:, 0:width].astype(BF)

    total = b_ref[...] + w_ref[TAPS - 1 : TAPS] * x.astype(F32)
    for lag in range(1, TAPS):
        value = dot(select(r - lag, pos >= lag, ROWS), x)
        for i in range(TAPS - 1):
            old = (pos == i + lag - 3) & (pos < lag) & (res > 0)
            value = value + dot(select(slot, old, SEQ), cache_ref[i])
        total = total + w_ref[TAPS - 1 - lag : TAPS - lag] * value
    cx = silu(total).astype(BF)
    cx_ref[...] = cx
    for copy in copies[7:]:
        copy.wait()
    proj_ref[0:ROWS, 0:512] = dot(cx, rank_ref[...]).astype(BF)
    proj_ref[0:ROWS, 512:640] = jnp.zeros((ROWS, 128), BF)
    proj_ref[0:ROWS, 512 : 512 + 2 * NS] = lax.dot_general(
        cx, sw_ref[...], (((1,), (1,)), ((), ())), preferred_element_type=F32
    ).astype(BF)
    line = 2 * (2 * lax.axis_index("x") + lax.axis_index("core"))
    inverse = 1.0 / (gain_ref[...] * gain_ref[...])
    high = inverse.astype(BF).astype(F32)
    row = iota((16, 512), 0)
    extra = jnp.where(row == line, high, jnp.where(row == line + 1, inverse - high, 0.0))
    proj_ref[ROWS : ROWS + 16, 0:512] = extra.astype(BF)
    proj_ref[ROWS : ROWS + 16, 512:640] = jnp.zeros((16, 128), BF)


def tail_kernel(span_ref, res_ref, slot_ref, x_ref, cache_ref, nc_ref):
    starts = span_starts(span_ref)
    x = x_ref[...]
    group = iota((SEQ, 128), 0)
    j = iota((SEQ, 128), 1)
    length = jnp.ones((SEQ, 128), I32)
    first = jnp.zeros((SEQ, 128), I32)
    kept = jnp.ones((SEQ, 128), I32)
    for s in range(SEQ):
        here = group == slot_ref[0, s]
        if s < DEC:
            first = jnp.where(here, s, first)
        else:
            first = jnp.where(here, starts[s - DEC], first)
            length = jnp.where(here, span_ref[0, s - DEC], length)
            kept = jnp.where(here, res_ref[0, s - DEC], kept)

    def select(column, line, width):
        return (j == jnp.where(line, column, -1)).astype(F32)[:, 0:width].astype(BF)

    for offset in range(TAPS - 1):
        back = length - (TAPS - 1) + offset
        value = dot(select(first + back, back >= 0, ROWS), x)
        for i in range(TAPS - 1):
            old = (back == i - 3) & (kept > 0)
            value = value + dot(select(group, old, SEQ), cache_ref[i])
        nc_ref[offset] = value.astype(BF)


def scan_kernel(
    here_ref, span_ref, res_ref, slot_ref,
    q0_ref, q1_ref, q2_ref, q3_ref, cx_ref, z_ref, gain_ref, sw_ref, sb_ref, dl_ref, skip_ref,
    sc_ref, ow_ref,
    ns_ref, own_ref, sib_ref, inv_ref,
    state_ref, w_vmem, step_ref, drive_ref, bb_ref, cb_ref, pc_ref, tr_ref, sem, state_sem,
):
    fetch = pltpu.make_async_copy(ow_ref, w_vmem, sem)
    fetch.start()
    starts = span_starts(span_ref)
    sums = (
        q0_ref[...].astype(F32) + q1_ref[...].astype(F32)
        + q2_ref[...].astype(F32) + q3_ref[...].astype(F32)
    )
    proj = sums[0:ROWS]
    for t in range(8):
        inverse = sums[ROWS + 2 * t : ROWS + 2 * t + 1, 0:512] + sums[ROWS + 2 * t + 1 : ROWS + 2 * t + 2, 0:512]
        inv_ref[t // 2, :, 512 * (t % 2) : 512 * (t % 2) + 512] = inverse
    low = proj[:, 0:512]
    mean = jnp.mean(low * low, axis=1, keepdims=True)
    norm = (low * lax.rsqrt(mean + EPS) * gain_ref[...]).astype(BF)
    pre = dot(norm, sw_ref[...]) + sb_ref[...]
    step = jnp.maximum(pre, 0.0) + jnp.log1p(jnp.exp(-jnp.abs(pre)))
    values = cx_ref[...].astype(F32)
    step_ref[...] = step
    drive_ref[...] = step * values
    tr_ref[0:ROWS] = proj[:, 512:640]
    tr_ref[ROWS : 2 * ROWS] = jnp.zeros((ROWS, 128), F32)
    turned = tr_ref[...].T
    for r in range(ROWS):
        bb_ref[r] = jnp.broadcast_to(turned[0:NS, r : r + 1], (NS, 128))
        cb_ref[r] = jnp.broadcast_to(turned[NS : 2 * NS, r : r + 1], (NS, 128))
    rate = -jnp.exp(dl_ref[...])
    groups = rate.shape[1] // 128

    def advance(r, state):
        c1 = (r >= starts[1]).astype(I32)
        c2 = (r >= starts[2]).astype(I32)
        c3 = (r >= starts[3]).astype(I32)
        piece = c1 + c2 + c3
        decode = r < DEC
        slot = slot_ref[0, jnp.where(decode, r, DEC + piece)]
        resumed = jnp.where(decode, 1, res_ref[0, piece])
        begins = (r <= DEC) | (r == starts[1]) | (r == starts[2]) | (r == starts[3])
        keep = jnp.where(begins, 0.0, 1.0).astype(F32)
        load = jnp.where(begins, resumed, 0).astype(F32)
        prior = state * keep + sc_ref[slot] * load
        decay = jnp.exp(step_ref[pl.ds(r, 1), :] * rate)
        b = jnp.concatenate([bb_ref[r]] * groups, axis=1)
        c = jnp.concatenate([cb_ref[r]] * groups, axis=1)
        fresh = decay * prior + drive_ref[pl.ds(r, 1), :] * b
        weighed = fresh * c
        pc_ref[r] = weighed[0:8] + weighed[8:16]
        state_ref[slot] = fresh
        return fresh

    lax.fori_loop(0, ROWS, advance, jnp.zeros(rate.shape, F32), unroll=4)
    keep = pltpu.make_async_copy(state_ref, ns_ref, state_sem)
    keep.start()
    output = skip_ref[...] * values
    for k in range(8):
        output = output + pc_ref[:, k, :]
    gated = (output * silu(z_ref[...].astype(F32))).astype(BF)
    fetch.wait()
    x, c = here_ref[0], here_ref[1]
    for out, core in ((own_ref, c), (sib_ref, 1 - c)):
        for k in range(4):
            cols = pl.ds(pl.multiple_of((2 * lax.rem(x + k, 4) + core) * 512, 512), 512)
            out[k] = dot(gated, w_vmem[:, cols]).astype(BF)
    keep.wait()


def pick_kernel(
    here_ref, q0_ref, q1_ref, q2_ref, q3_ref, resid_ref, gain_ref, router_ref, chosen_ref,
    hid_ref, mine_ref, theirs_ref, named_ref,
):
    mixer = (
        q0_ref[...].astype(F32) + q1_ref[...].astype(F32)
        + q2_ref[...].astype(F32) + q3_ref[...].astype(F32)
    ).astype(BF)
    hidden = resid_ref[...].astype(F32) + mixer.astype(F32)
    hid_ref[...] = hidden
    scaled = (hidden * gain_ref[...]).astype(BF)
    wide = scaled.astype(F32)
    lane = iota((ROWS, 128), 1)
    squares = jnp.sum(hidden * hidden, axis=1, keepdims=True)
    stat = jnp.where(lane % 64 == EXPERTS, squares, 0.0)
    for e in range(EXPERTS):
        part = jnp.sum(wide * router_ref[e : e + 1].astype(F32), axis=1, keepdims=True)
        stat = jnp.where(lane % 64 == e, part, stat)
    high = stat.astype(BF).astype(F32)
    stat = jnp.where(lane < 64, high, stat - high).astype(BF)
    for out in (mine_ref, theirs_ref):
        out[0, :, 512:640] = stat[0:CAP]
        out[1, :, 512:640] = jnp.concatenate([stat[CAP:ROWS], jnp.zeros((2 * CAP - ROWS, 128), BF)], axis=0)
    before = (iota((ROWS, ROWS), 0) < iota((ROWS, ROWS), 1)).astype(F32).astype(BF)
    row = iota((CAP, ROWS), 0)
    z, core = here_ref[2], here_ref[1]
    expert = lax.rem(z + 2 * core + iota((8, ROWS), 0), EXPERTS)
    marks = ((chosen_ref[0:1] == expert) | (chosen_ref[1:2] == expert)).astype(F32)
    place = dot(marks.astype(BF), before)
    place = jnp.where(marks > 0.0, place, -1.0).astype(I32)
    for i in range(4):
        hot = (row == place[i : i + 1]).astype(F32).astype(BF)
        out = mine_ref if i < 2 else theirs_ref
        out[i % 2, :, 0:512] = dot(hot, scaled).astype(BF)
    same = (iota((ROWS, ROWS), 0) == iota((ROWS, ROWS), 1)).astype(F32).astype(BF)
    pair = iota((8, ROWS), 0)
    both = jnp.where(pair == 0, chosen_ref[0:1], jnp.where(pair == 1, chosen_ref[1:2], 0))
    turned = lax.dot_general(
        same, both.astype(F32).astype(BF), (((1,), (1,)), ((), ())), preferred_element_type=F32
    )
    named_ref[...] = jnp.zeros_like(named_ref)
    named_ref[:, 0:8] = turned.astype(I32)


def experts_in(here_ref, side, x_ref, inv_ref, wg_ref, wu_ref):
    x = here_ref[0]
    by_row, by_col = jnp.where(side == 0, 4, 1), jnp.where(side == 0, 1, 4)
    both = square = None
    for k in range(4):
        there = lax.rem(x + 4 - k, 4)
        rows = pl.ds(pl.multiple_of(there * 1024, 1024), 1024)
        block = jnp.concatenate([x_ref[j * by_row + k * by_col] for j in range(4)], axis=0)
        part = dot(block, jnp.concatenate([wg_ref[rows, :], wu_ref[rows, :]], axis=1))
        wide = block.astype(F32)
        wide = wide * wide * inv_ref[there]
        square_part = wide[:, 0:128]
        for lane in range(128, 1024, 128):
            square_part = square_part + wide[:, lane : lane + 128]
        if k == 0:
            both, square = part, square_part
        else:
            both, square = both + part, square + square_part
    both = both * lax.rsqrt(jnp.sum(square, axis=1, keepdims=True) / 4096.0 + EPS)
    return (silu(both[:, 0:384]) * both[:, 384:768]).astype(BF)


def experts_out(here_ref, side, act_ref, wd_ref, outs):
    x = here_ref[0]

    def product(rows, there):
        cols = pl.ds(pl.multiple_of(there * 1024, 1024), 1024)
        return dot(rows, wd_ref[:, cols]).astype(BF)

    @pl.when(side == 0)
    def _():
        owners = [j for j in range(4) if (4 - j) % 4 in outs]
        rows = jnp.concatenate([act_ref[96 * j : 96 * j + 96, :] for j in owners], axis=0)
        for n in range(4):
            value = product(rows, lax.rem(x + n, 4))
            for i, j in enumerate(owners):
                outs[(4 - j) % 4][n] = value[96 * i : 96 * i + 96]

    @pl.when(side == 1)
    def _():
        for m in outs:
            value = product(act_ref[...], lax.rem(x + m, 4))
            for j in range(4):
                outs[m][(4 - j) % 4] = value[96 * j : 96 * j + 96]


def gather_in(here_ref, terms, inv_ref, wg_ref, wu_ref):
    both = square = None
    for k, blocks in terms:
        there = lax.rem(here_ref[0] + 4 - k, 4)
        rows = pl.ds(pl.multiple_of(there * 1024, 1024), 1024)
        block = jnp.concatenate(blocks, axis=0)
        part = dot(block, jnp.concatenate([wg_ref[rows, :], wu_ref[rows, :]], axis=1))
        wide = block.astype(F32)
        wide = wide * wide * inv_ref[there]
        square_part = wide[:, 0:128]
        for lane in range(128, 1024, 128):
            square_part = square_part + wide[:, lane : lane + 128]
        if both is None:
            both, square = part, square_part
        else:
            both, square = both + part, square + square_part
    return both, square


def activate(both, square):
    both = both * lax.rsqrt(jnp.sum(square, axis=1, keepdims=True) / 4096.0 + EPS)
    return (silu(both[:, 0:384]) * both[:, 384:768]).astype(BF)


def ffn_early(here_ref, x_ref, inv_ref, wg_ref, wu_ref, wd_ref, acc_ref, sq_ref):
    weights = (inv_ref, wg_ref, wu_ref)

    @pl.when(here_ref[1] == 0)
    def _():
        terms = [(k, [x_ref[4 * i + k] for i in range(3)]) for k in range(4)]
        both, square = gather_in(here_ref, terms, *weights)
        for out, value in ((acc_ref, both), (sq_ref, square)):
            out[0:192] = value[0:192]
            out[192:288] = jnp.zeros_like(value[0:96])
            out[288:384] = value[192:288]

    @pl.when(here_ref[1] == 1)
    def _():
        terms = [(k, [x_ref[4 * i + n] for n in range(4)]) for i, k in enumerate((0, 1, 3))]
        acc_ref[...], sq_ref[...] = gather_in(here_ref, terms, *weights)


def ffn_late(here_ref, x_ref, inv_ref, wg_ref, wu_ref, acc_ref, sq_ref, act_ref):
    weights = (inv_ref, wg_ref, wu_ref)

    @pl.when(here_ref[1] == 0)
    def _():
        terms = [(k, [x_ref[k]]) for k in range(4)]
        both, square = gather_in(here_ref, terms, *weights)
        act_ref[0:192] = activate(acc_ref[0:192], sq_ref[0:192])
        act_ref[192:288] = activate(both, square)
        act_ref[288:384] = activate(acc_ref[288:384], sq_ref[288:384])

    @pl.when(here_ref[1] == 1)
    def _():
        both, square = gather_in(here_ref, [(2, [x_ref[n] for n in range(4)])], *weights)
        act_ref[...] = activate(acc_ref[...] + both, sq_ref[...] + square)


def ffn_own(here_ref, act_ref, wd_ref, p0_ref, p1_ref, p2_ref, p3_ref):
    experts_out(here_ref, here_ref[1], act_ref, wd_ref, {0: p0_ref, 1: p1_ref, 2: p2_ref, 3: p3_ref})


def ffn_other(
    here_ref, x_ref, inv_ref, wg_ref, wu_ref, wd_ref, earlier_ref,
    p0_ref, p1_ref, p2_ref, p3_ref, act_ref,
):
    side = 1 - here_ref[1]
    act_ref[...] = experts_in(here_ref, side, x_ref, inv_ref, wg_ref, wu_ref)
    experts_out(here_ref, side, act_ref, wd_ref, {0: p0_ref, 1: p1_ref, 2: p2_ref, 3: p3_ref})


def final_kernel(
    here_ref, mine_ref, theirs_ref, stat_ref, hid_ref, chosen_ref, out_ref,
):
    stat = stat_ref[0:ROWS].astype(F32)

    def column(e):
        return stat[:, e : e + 1] + stat[:, 64 + e : 65 + e]

    scale = lax.rsqrt(column(EXPERTS) / 4096.0 + EPS)
    e0, e1 = chosen_ref[:, 0:1], chosen_ref[:, 1:2]
    l0 = jnp.zeros((ROWS, 1), F32)
    l1 = jnp.zeros((ROWS, 1), F32)
    for e in range(EXPERTS):
        l0 = l0 + jnp.where(e0 == e, column(e), 0.0)
        l1 = l1 + jnp.where(e1 == e, column(e), 0.0)
    gap = (l0 - l1) * scale
    route0 = 1.0 / (1.0 + jnp.exp(-gap))
    route1 = 1.0 / (1.0 + jnp.exp(gap))
    before = (iota((ROWS, ROWS), 1) < iota((ROWS, ROWS), 0)).astype(F32).astype(BF)
    lane = iota((ROWS, CAP), 1)
    total = hid_ref[...]
    z, core = here_ref[2], here_ref[1]
    expert = lax.rem(z + 2 * core + iota((ROWS, 128), 1), EXPERTS)
    first, second = e0 == expert, e1 == expert
    marks = (first | second).astype(F32)
    place = dot(before, marks.astype(BF))
    place = jnp.where(marks > 0.0, place, -1.0).astype(I32)
    weight = jnp.where(first, route0, jnp.where(second, route1, 0.0))
    for i in range(4):
        hot = (lane == place[:, i : i + 1]).astype(F32).astype(BF)
        ref = mine_ref if i < 2 else theirs_ref
        total = total + weight[:, i : i + 1] * dot(hot, ref[i % 2])
    out_ref[...] = total.astype(BF)


def move(value, axis, shift):
    size = lax.axis_size(axis)
    return lax.ppermute(value, axis, [(i, (i + shift) % size) for i in range(size)])


def by_core(value, first, second):
    sizes = tuple(lax.axis_size(name) for name in AXES)
    pairs = []
    for source in range(int(np.prod(sizes))):
        place = list(np.unravel_index(source, sizes))
        axis, shift = (first, second)[int(place[3])]
        at = AXES.index(axis)
        place[at] = (place[at] + shift) % sizes[at]
        pairs.append((source, int(np.ravel_multi_index(place, sizes))))
    return lax.ppermute(value, AXES, pairs)


def across(value, shift):
    return by_core(value, ("x", shift), ("y", shift))


def along(value, shift):
    return by_core(value, ("y", shift), ("x", shift))


def summed(*values):
    total = values[0].astype(F32)
    for value in values[1:]:
        total = total + value.astype(F32)
    return total[..., 0:64] + total[..., 64:128]


def coded(value):
    high = value.astype(BF)
    low = (value - high.astype(F32)).astype(BF)
    return jnp.concatenate([high, low], axis=-1)


def add(*values):
    total = values[0].astype(F32)
    for value in values[1:]:
        total = total + value.astype(F32)
    return total.astype(BF)


def stay(value):
    return pltpu.with_memory_space_constraint(value, pltpu.HBM)


def call(kernel, outs, ins, mib, scratch=(), flops=0, moved=0, name=None, out_specs=None):
    single = not isinstance(outs, (list, tuple))
    return pl.pallas_call(
        kernel,
        out_shape=outs,
        in_specs=ins,
        out_specs=out_specs or (VMEM if single else [VMEM] * len(outs)),
        scratch_shapes=list(scratch),
        compiler_params=params(mib),
        cost_estimate=pl.CostEstimate(flops=flops, bytes_accessed=moved, transcendentals=0),
        name=name,
    )


def shape(dims, dtype):
    return jax.ShapeDtypeStruct(dims, dtype)


def per_device(
    conv_input, gate_input, conv_cache, state_cache, span_lengths, span_resumes, slot_index,
    conv_weight, conv_bias, rank_weight, state_weight, step_gain, step_weight, step_bias,
    decay_log, skip_gain, out_weight, residual, moe_gain, router_weight, chosen_experts,
    gate_weight, up_weight, down_weight,
):
    here = jnp.stack(
        [lax.axis_index("x"), lax.axis_index("core"), lax.axis_index("z")]
    ).astype(I32)
    even = lax.axis_index("core") == 0
    old = conv_cache.transpose(1, 0, 2)
    cx, proj = call(
        conv_kernel,
        [shape((ROWS, 1024), BF), shape((ROWS + 16, 640), BF)],
        [HBM] * 10,
        16,
        [
            pltpu.SMEM((1, 4), I32),
            pltpu.SMEM((1, 4), I32),
            pltpu.SMEM((1, SEQ), I32),
            pltpu.VMEM((ROWS, 1024), BF),
            pltpu.VMEM((3, SEQ, 1024), BF),
            pltpu.VMEM((TAPS, 1024), F32),
            pltpu.VMEM((1, 1024), F32),
            pltpu.VMEM((1024, 512), BF),
            pltpu.VMEM((2 * NS, 1024), BF),
            pltpu.VMEM((1, 512), F32),
            pltpu.SemaphoreType.DMA((10,)),
        ],
        flops=10**9,
        moved=2 * 10**6,
        name="conv",
    )(
        *map(
            stay,
            (
                span_lengths, span_resumes, slot_index, conv_input,
                old, conv_weight, conv_bias.reshape(1, 1024),
                rank_weight, state_weight.T, moe_gain.reshape(1, 512),
            ),
        )
    )
    new_conv = call(
        tail_kernel,
        shape((3, SEQ, 1024), BF),
        [SMEM] * 3 + [VMEM] * 2,
        8,
        flops=10**9,
        moved=10**6,
        name="tail",
    )(span_lengths, span_resumes, slot_index, conv_input, old)
    chip = add(proj, move(proj, "core", 1))
    parts = [chip] + [move(chip, "x", k) for k in (1, 2, 3)]
    new_state, own, sib, inverse = call(
        scan_kernel,
        [
            shape((SEQ, NS, 1024), F32),
            shape((4, ROWS, 512), BF),
            shape((4, ROWS, 512), BF),
            shape((4, 1, 1024), F32),
        ],
        [SMEM] * 4 + [VMEM] * 12 + [HBM],
        32,
        [
            pltpu.VMEM((SEQ, NS, 1024), F32),
            pltpu.VMEM((1024, 4096), BF),
            pltpu.VMEM((ROWS, 1024), F32),
            pltpu.VMEM((ROWS, 1024), F32),
            pltpu.VMEM((ROWS, NS, 128), F32),
            pltpu.VMEM((ROWS, NS, 128), F32),
            pltpu.VMEM((ROWS, 8, 1024), F32),
            pltpu.VMEM((128, 128), F32),
            pltpu.SemaphoreType.DMA,
            pltpu.SemaphoreType.DMA,
        ],
        flops=10**9,
        moved=10**7,
        name="scan",
        out_specs=[HBM] + [VMEM] * 3,
    )(
        here, span_lengths, span_resumes, slot_index, *parts, cx, gate_input,
        step_gain.reshape(1, 512), step_weight, step_bias.reshape(1, 1024), decay_log,
        skip_gain.reshape(1, 1024), state_cache, stay(out_weight),
    )
    mixed = add(own, move(sib, "core", 1))
    parts = [mixed[0]] + [move(mixed[k], "x", k) for k in (1, 2, 3)]
    hidden, mine, theirs, named = call(
        pick_kernel,
        [
            shape((ROWS, 512), F32),
            shape((2, CAP, 640), BF),
            shape((2, CAP, 640), BF),
            shape((ROWS, 128), I32),
        ],
        [SMEM] + [VMEM] * 8,
        8,
        flops=10**8,
        moved=10**6,
        name="pick",
    )(here, *parts, residual, moe_gain.reshape(1, 512), router_weight.T, chosen_experts.T)
    theirs = move(theirs, "core", 1)
    stat = coded(summed(mine[:, :, 512:640], theirs[:, :, 512:640])).reshape(2 * CAP, 128)
    mine, theirs = mine[:, :, 0:512], theirs[:, :, 0:512]
    rows = jnp.concatenate([jnp.where(even, mine, theirs), jnp.where(even, theirs, mine)], axis=2)
    later = by_core(rows[1], ("z", 1), ("z", 3))
    sooner = by_core(rows[0], ("z", 0), ("z", 2))
    rows = jnp.concatenate([jnp.concatenate([sooner, later], axis=0), stat], axis=1)
    rows1, rows3 = across(rows, 1), across(rows, 3)
    rows2 = jnp.concatenate([across(rows1[0:CAP], 1), across(rows3[CAP : 2 * CAP], 3)], axis=0)
    stat = coded(summed(*[part[:, 1024:1152] for part in (rows, rows1, rows2, rows3)]))
    early = jnp.stack([part[:, 0:1024] for part in (rows, rows1, rows3)])
    late = rows2[None, :, 0:1024]
    early1, early3 = along(early, 1), along(early, 3)
    late1, late3 = along(late, 1), along(late, 3)
    early2 = along(early1[0:2], 1), along(early3[2:3], 3)
    late2 = along(late3, 3)
    most = jnp.concatenate(
        [
            early[0:2], late, early[2:3], early1[0:2], late1, early1[2:3],
            early3[0:2], late3, early3[2:3],
        ],
        axis=0,
    )
    last = jnp.concatenate([early2[0], late2, early2[1]], axis=0)
    their_most = move(most, "core", 1)
    gate, up, down = gate_weight[0], up_weight[0], down_weight[0]
    block = shape((4, 96, 1024), BF)

    acc, square = call(
        ffn_early,
        [shape((384, 768), F32), shape((384, 128), F32)],
        [SMEM] + [VMEM] * 5,
        20,
        flops=2 * 288 * 4096 * 768,
        moved=8 * 10**6,
        name="experts_early",
    )(here, most, inverse, gate, up, down)
    last, acc = lax.optimization_barrier((last, acc))
    their_last = move(last, "core", 1)
    own = call(
        ffn_late,
        shape((384, 384), BF),
        [SMEM] + [VMEM] * 6,
        16,
        flops=2 * 96 * 4096 * 768,
        moved=8 * 10**6,
        name="experts_late",
    )(here, last, inverse, gate, up, acc, square)
    theirs = jnp.concatenate([their_most[0:8], their_last, their_most[8:12]], axis=0)
    theirs = call(
        ffn_other,
        [block] * 4,
        [SMEM] + [VMEM] * 6,
        24,
        [pltpu.VMEM((384, 384), BF)],
        flops=6 * 384 * 2048 * 768,
        moved=10 * 10**6,
        name="experts_other",
    )(here, theirs, inverse, gate, up, down, own)
    mine = call(
        ffn_own,
        [block] * 4,
        [SMEM] + [VMEM] * 2,
        13,
        flops=384 * 4096 * 768,
        moved=5 * 10**6,
        name="experts_own",
    )(here, own, down)
    part2 = add(mine[2], move(theirs[2], "core", 1))
    far1, far3 = along(part2[0:2], 1), along(part2[2:4], 3)
    part1 = add(mine[1], move(theirs[1], "core", 1))
    part3 = add(mine[3], move(theirs[3], "core", 1))
    part0 = add(mine[0], move(theirs[0], "core", 1))
    near1, near3 = along(part1[2:4], 1), along(part3[0:2], 3)
    next1, next3 = along(add(part1[0:2], far1), 1), along(add(part3[2:4], far3), 3)
    lines = jnp.concatenate(
        [add(part0[0:2], next1, near3), add(part0[2:4], near1, next3)], axis=0
    )
    lines = add(lines[0], *[across(lines[k], k) for k in (1, 2, 3)])
    later = by_core(lines[CAP : 2 * CAP], ("z", 3), ("z", 1))
    sooner = by_core(lines[0:CAP], ("z", 0), ("z", 2))
    lines = jnp.stack([sooner, later])
    left, right = lines[:, :, 0:512], lines[:, :, 512:1024]
    mine = jnp.where(even, left, right)
    theirs = jnp.concatenate([jnp.where(even, right, left), stat.reshape(2, CAP, 128)], axis=2)
    theirs = move(theirs, "core", 1)
    stat = jnp.where(even, stat, theirs[:, :, 512:640].reshape(2 * CAP, 128))
    theirs = theirs[:, :, 0:512]
    out = call(
        final_kernel,
        shape((ROWS, 512), BF),
        [SMEM] + [VMEM] * 5,
        8,
        flops=10**8,
        moved=10**6,
        name="combine",
    )(here, mine, theirs, stat, hidden, named)
    new_conv = new_conv.transpose(1, 0, 2)
    return (out, new_state, new_conv)


def solution(mesh):
    grid = Mesh(mesh.devices.reshape(4, 4, 4, 2), AXES)
    group, tensor = ("z", "y"), ("x", "core")
    return jax.shard_map(
        per_device,
        mesh=grid,
        in_specs=(
            P(group, tensor),
            P(group, tensor),
            P(group, None, tensor),
            P(group, None, tensor),
            P(group, None),
            P(group, None),
            P(group, None),
            P(None, tensor),
            P(tensor),
            P(tensor, None),
            P(tensor, None),
            P(),
            P(None, tensor),
            P(tensor),
            P(None, tensor),
            P(tensor),
            P(tensor, None),
            P(group, tensor),
            P(tensor),
            P(tensor, None),
            P(group, None),
            P(group, None, tensor),
            P(group, None, tensor),
            P(group, tensor, None),
        ),
        out_specs=(P(group, tensor), P(group, None, tensor), P(group, None, tensor)),
        check_vma=False,
    )
```
